512 devices in a mesh: ka: 32 (over z, x_lo), pw: 16 (over x_hi, y, core).
Axes of the slice: x: 4 (x_hi: 2, x_lo: 2; x = x_hi * 2 + x_lo), y: 4, z: 16, core: 2. Of those that a mesh axis runs over, the one named last changes fastest.
Arguments:
- wave: bfloat16 [32, 2, 256, 20480], P('ka', None, None, 'pw'), may hold values from -0.4375 to 0.4375
- wave_perm: int32 [32, 3, 20480], P('ka', None, 'pw'), may hold values from 0 to 20479, as said below
- shell_weight: float32 [3], replicated, may hold values from 0.25 to 1
Outputs:
- correlation: float32 [32, 3, 2, 256, 256], P('ka', None, None, 'pw')
- gradient: float32 [32, 2, 256, 256], P('ka')
The draws below stay inside these ranges and needn't reach their ends.
Inputs may be any that keep to these rules, and one draw needn't show every extreme that they name: Each list wave_perm[k, d, :] is a permutation of the 20480 plane waves that maps every aligned block of 1280 rows onto itself.
All inputs are finite; a program needn't handle non-finite values.
Results may differ from the reference program's by a relative error of at most 0.0003.
Values may be sent and summed in bfloat16 or wider, within the bound.
A program may use at most 64 MiB of HBM per device.

```python
import math
import jax
import jax.numpy as jnp
from jax import lax

NB = 256
NPW = 20480
NKY = 4
NKZ = 2
NK = 32
NKX = 4
PW_DEV = 1280


def draw_wave_perm(key, part):
    key = jax.random.fold_in(key, 7)
    block_count = NPW // PW_DEV
    base = jnp.broadcast_to(jnp.arange(PW_DEV, dtype=jnp.int32), (NK * 3 * block_count, PW_DEV))
    mixed = jax.random.permutation(key, base, axis=1, independent=True)
    offsets = (jnp.arange(block_count, dtype=jnp.int32) * PW_DEV)[None, :, None]
    return (mixed.reshape(NK * 3, block_count, PW_DEV) + offsets).reshape(NK, 3, NPW).astype(jnp.int32)


def block_levels(stream_key, extent, shards, low, top_value):
    def one(dim, shards_of):
        heights = jax.random.uniform(jax.random.fold_in(jax.random.fold_in(stream_key, 6), dim), (shards_of,), jnp.float32, low / len(shards), top_value / len(shards))
        return jnp.repeat(jnp.exp(heights), extent[dim] // shards_of).reshape((-1,) + (1,) * (len(extent) - dim - 1))

    level = one(*shards[0])
    for cut in shards[1:]:
        level = level * one(*cut)
    return level


def noise(own_key, shape, scale, most, shards=(), kind=jnp.bfloat16):
    values = jax.random.normal(own_key, shape, jnp.float32) * scale
    if len(shards) > 0:
        values = block_levels(own_key, shape, shards, -0.22, 0.18) * values
    return jnp.clip(values, min=-most, max=most).astype(kind)


def setup_inputs(seed: int = 0) -> dict:
    arg_keys = jax.random.split(jax.random.key(seed), 4)
    return {
        "wave": noise(arg_keys[0], (NK, 2, NB, NPW), ((2 * NPW) ** -0.25), 0.4375, ((0, 32), (3, 16))),
        "wave_perm": draw_wave_perm(jax.random.fold_in(arg_keys[3], 71), 0),
        "shell_weight": jnp.clip(jnp.exp(jax.random.uniform(arg_keys[2], (3,), jnp.float32, math.log(0.25), math.log(1.0))), 0.25, 1.0),
    }


def correlation_of(current, other):
    real_real = jnp.dot(current[0], other[0].T, preferred_element_type=jnp.float32)
    imag_imag = jnp.dot(current[1], other[1].T, preferred_element_type=jnp.float32)
    real_imag = jnp.dot(current[0], other[1].T, preferred_element_type=jnp.float32)
    imag_real = jnp.dot(current[1], other[0].T, preferred_element_type=jnp.float32)
    return jnp.stack([real_real + imag_imag, real_imag - imag_real])


def skew_part(real_part, imag_part):
    diag_real = jnp.diagonal(real_part)
    diag_imag = jnp.diagonal(imag_part)
    rot_real = real_part * diag_real[None, :] + imag_part * diag_imag[None, :]
    rot_imag = imag_part * diag_real[None, :] - real_part * diag_imag[None, :]
    return 0.5 * (rot_real - rot_real.T), 0.5 * (rot_imag + rot_imag.T)


def mesh_tables():
    points = jnp.arange(NK, dtype=jnp.int32)
    first_pos = points // (NKY * NKZ)
    second_pos = (points // NKZ) % NKY
    third_pos = points % NKZ

    def index_of(first, second, third):
        return (((first % NKX) * NKY + second % NKY) * NKZ + third % NKZ).astype(jnp.int32)

    ahead = jnp.stack([index_of(first_pos + 1, second_pos, third_pos),
                       index_of(first_pos, second_pos + 1, third_pos),
                       index_of(first_pos, second_pos, third_pos + 1)])
    behind = jnp.stack([index_of(first_pos + NKX - 1, second_pos, third_pos),
                        index_of(first_pos, second_pos + NKY - 1, third_pos),
                        index_of(first_pos, second_pos, third_pos + NKZ - 1)])
    return ahead, behind


def reference(wave, wave_perm, shell_weight):
    ahead, behind = mesh_tables()

    def one_point(point):
        current = wave[point]
        matrices = []
        for direction in range(3):
            other = jnp.take(wave[ahead[direction, point]], wave_perm[point, direction], axis=2)
            matrices.append(correlation_of(current, other))
        return jnp.stack(matrices)

    correlation = lax.map(one_point, jnp.arange(NK, dtype=jnp.int32))

    def one_gradient(point):
        grad_real = jnp.zeros((NB, NB), jnp.float32)
        grad_imag = jnp.zeros((NB, NB), jnp.float32)
        for direction in range(3):
            forward_mat = correlation[point, direction]
            back_mat = correlation[behind[direction, point], direction]
            ahead_real, ahead_imag = skew_part(forward_mat[0], forward_mat[1])
            back_real, back_imag = skew_part(back_mat[0].T, -back_mat[1].T)
            grad_real = grad_real + shell_weight[direction] * (ahead_real + back_real)
            grad_imag = grad_imag + shell_weight[direction] * (ahead_imag + back_imag)
        return jnp.stack([grad_real, grad_imag])

    gradient = lax.map(one_gradient, jnp.arange(NK, dtype=jnp.int32))
    return correlation, gradient
```

```python
import jax
import jax.numpy as jnp
from jax import lax
from jax.experimental import pallas as pl
from jax.experimental.pallas import tpu as pltpu
from jax.sharding import PartitionSpec as P

MESH = pl.DeviceIdType.MESH
NK = 32
NB = 256
NG = 1280
NQ = 8
HOPS = 4
CHUNKS = 4
ROWS = NB // CHUNKS
A, B, W, C = range(4)
BLOCK = 72
HALF = 40


def kernel(
    wave, perm, weight, corr_out, grad_out,
    stream, other, turned, product, lists, part, gathered, reduced, ends, zrows,
    stream_send, stream_recv, other_send, other_recv, list_send, list_recv,
    part_send, part_recv, end_send, end_recv, z_send, z_recv, zz_send, zz_recv,
):
    k = lax.axis_index("ka")
    p = lax.axis_index("pw")
    core = p % 2
    q = p // 2
    sibling = p + 1 - 2 * core
    level = k // 2 % 4
    group = k // 8 * 8
    inner = k % 8
    to_next = (k + 30 + 4 * core) % NK
    a_up, a_down = (k + 8) % NK, (k + 24) % NK
    b_up, b_down = group + (inner + 2) % 8, group + (inner + 6) % 8
    flip = k + 1 - 2 * (k % 2)
    a_end = (k + 8 + 16 * core) % NK
    b_end = group + (inner + 2 + 4 * core) % 8
    w_end = group + (inner + 6 - 4 * core) % 8
    b_here = level != 3 - 3 * core
    w_here = level == 3 * core

    def remote(src, dst, send_sem, recv_sem, ka, pw):
        return pltpu.make_async_remote_copy(
            src_ref=src, dst_ref=dst, send_sem=send_sem, recv_sem=recv_sem,
            device_id=(ka, pw), device_id_type=MESH,
        )

    barrier = pltpu.get_barrier_semaphore()
    peers = [((k + 2) % NK, p), ((k + 30) % NK, p), (k, sibling)]
    for end in (a_up, a_down, b_up, b_down, flip):
        peers += [(end, 2 * q), (end, 2 * q + 1)]
    peers += [(k, (q + j) % NQ * 2 + core) for j in range(1, NQ)]
    for peer in peers:
        pl.semaphore_signal(barrier, inc=1, device_id=peer, device_id_type=MESH)
    pl.semaphore_wait(barrier, len(peers))

    def own_copy(c):
        rows = pl.ds(pl.multiple_of(c * ROWS, ROWS), ROWS)
        return remote(
            wave.at[:, rows, :], stream.at[0, :, rows, :],
            stream_send.at[0, c], stream_recv.at[0, c], to_next, p,
        )

    def hop_copy(h, c):
        rows = pl.ds(pl.multiple_of(c * ROWS, ROWS), ROWS)
        return remote(
            stream.at[h - 1, :, rows, :], stream.at[h, :, rows, :],
            stream_send.at[h, c], stream_recv.at[h, c], to_next, p,
        )

    def list_copy(i):
        return remote(
            perm, lists.at[i + 1], list_send.at[i], list_recv.at[i], (a_up, b_up)[i], p
        )

    other_copy = remote(wave, other, other_send, other_recv, flip, p)

    list_copy(0).start()
    list_copy(1).start()

    @pl.loop(0, CHUNKS)
    def _(c):
        own_copy(c).start()

    other_copy.start()
    lists[0] = perm[...]
    list_copy(0).wait_recv()
    list_copy(1).wait_recv()

    def turn(slot):
        which = (1 - core) * 2 * (slot // 2) * (1 - slot % 2) + core * ((slot + 1) % 3) * (1 - slot // 2)
        direction = (slot + 1) // 2
        at_start = (1 - core) * (1 - slot // 2 * (1 - slot % 2)) + core * (slot // 2)

        @pl.when(at_start == 1)
        def _():
            @pl.loop(0, NG // 256)
            def _(j):
                row = lists[which, direction] - p * NG
                wanted = lax.broadcasted_iota(jnp.int32, (256, NG), 0) + j * 256
                pick = jnp.where(wanted == row, 1.0, 0.0).astype(jnp.bfloat16)
                value = lax.dot_general(
                    wave[...].reshape(2 * NB, NG), pick, (((1,), (1,)), ((), ())),
                    preferred_element_type=jnp.float32,
                )
                turned[slot, :, pl.ds(pl.multiple_of(j * 256, 256), 256)] = value.astype(jnp.bfloat16)

        @pl.when(at_start == 0)
        def _():
            @pl.loop(0, NG // 256)
            def _(j):
                columns = pl.ds(pl.multiple_of(j * 256, 256), 256)
                row = lists[which, direction, :, columns] - p * NG
                held = lax.broadcasted_iota(jnp.int32, (NG, 256), 0)
                pick = jnp.where(held == row, 1.0, 0.0).astype(jnp.bfloat16)
                value = lax.dot_general(
                    wave[...].reshape(2 * NB, NG), pick, (((1,), (0,)), ((), ())),
                    preferred_element_type=jnp.float32,
                )
                turned[slot, :, columns] = value.astype(jnp.bfloat16)

    def multiply(slot, source, c):
        rows = pl.ds(pl.multiple_of(c * ROWS, ROWS), ROWS)
        value = lax.dot_general(
            source[:, rows, :].reshape(2 * ROWS, NG), turned[slot], (((1,), (1,)), ((), ())),
            preferred_element_type=jnp.float32,
        )
        product[0, rows, :] = value[:ROWS, :NB] + value[ROWS:, NB:]
        product[1, rows, :] = value[:ROWS, NB:] - value[ROWS:, :NB]

    def part_copy(slot, j):
        dest = (q + j) % NQ
        return remote(
            part.at[slot, dest], gathered.at[slot, j],
            part_send.at[slot, j], part_recv.at[slot, j], k, dest * 2 + core,
        )

    def hand_out(slot, at_start):
        swap = jnp.broadcast_to(at_start, (NB, NB)) > 0
        real, imag = product[0], product[1]
        real = jnp.where(swap, real.T, real)
        imag = jnp.where(swap, -imag.T, imag)
        eye = lax.broadcasted_iota(jnp.int32, (NB, NB), 0) == lax.broadcasted_iota(jnp.int32, (NB, NB), 1)
        diag_real = jnp.sum(jnp.where(eye, real, 0.0), axis=0, keepdims=True)
        diag_imag = jnp.sum(jnp.where(eye, imag, 0.0), axis=0, keepdims=True)
        first = lax.broadcasted_iota(jnp.int32, (8, NB), 0) < 4
        diag = jnp.where(first, diag_real, diag_imag)
        real = real.reshape(NQ, 2, 16, NB)
        imag = imag.reshape(NQ, 2, 16, NB)
        part[slot, :, 0:16, :] = real[:, 0]
        part[slot, :, 16:32, :] = imag[:, 0]
        part[slot, :, 32:48, :] = real[:, 1]
        part[slot, :, 48:64, :] = imag[:, 1]
        part[slot, :, 64:72, :] = jnp.broadcast_to(diag[None], (NQ, 8, NB))

        @pl.loop(1, NQ)
        def _(j):
            part_copy(slot, j).start()

    def end_copies(slot):
        if slot == C:
            direction, role, far_role, end, near, far = 2, 0, 1, flip, core, core
        elif slot == W:
            direction, role, far_role, end, near, far = 1, 1 - core, core, w_end, 0, 1
        else:
            direction, role, far_role, end, near, far = slot, core, 1 - core, (a_end, b_end)[slot], 0, 1
        local = (direction, role, near)
        target = ends.at[direction, far_role, far]
        sem = end_recv.at[direction, far_role, far]
        copies = [
            remote(
                reduced.at[slot, 1 - core], ends.at[direction, role, near],
                end_send.at[slot, 0], end_recv.at[direction, role, near], k, sibling,
            ),
            remote(reduced.at[slot, 0], target, end_send.at[slot, 1], sem, end, 2 * q),
            remote(reduced.at[slot, 1], target, end_send.at[slot, 2], sem, end, 2 * q + 1),
        ]
        return local, copies

    def pass_on(slot):
        @pl.loop(1, NQ)
        def _(j):
            part_copy(slot, j).wait_recv()

        total = part[slot, q]
        for j in range(1, NQ):
            total = total + gathered[slot, j]
        reduced[slot, 0, 0:32, :] = total[0:32]
        reduced[slot, 0, 32:40, :] = total[64:72]
        reduced[slot, 1, 0:32, :] = total[32:64]
        reduced[slot, 1, 32:40, :] = total[64:72]
        local, copies = end_copies(slot)
        for copy in copies:
            copy.start()
        ends[local[0], local[1], local[2]] = reduced[slot, core]

    @pl.loop(0, CHUNKS)
    def _(c):
        turn(3 - c)
        own_copy(c).wait_recv()
        hop_copy(1, c).start()

    @pl.when(b_here)
    def _():
        @pl.loop(0, CHUNKS)
        def _(c):
            multiply(B, stream.at[0], c)

        hand_out(B, 1 - core)

    @pl.loop(0, CHUNKS)
    def _(c):
        hop_copy(1, c).wait_recv()
        hop_copy(2, c).start()

    other_copy.wait_recv()

    @pl.loop(0, CHUNKS)
    def _(c):
        multiply(C, other, c)

    hand_out(C, 1)

    @pl.loop(0, CHUNKS)
    def _(c):
        hop_copy(2, c).wait_recv()
        hop_copy(3, c).start()

    @pl.when(w_here)
    def _():
        @pl.loop(0, CHUNKS)
        def _(c):
            multiply(W, stream.at[2], c)

        hand_out(W, core)

    @pl.when(b_here)
    def _():
        pass_on(B)

    pass_on(C)

    @pl.loop(0, CHUNKS // 2)
    def _(c):
        hop_copy(3, c).wait_recv()
        multiply(A, stream.at[3], c)

    @pl.when(w_here)
    def _():
        pass_on(W)

    @pl.loop(CHUNKS // 2, CHUNKS)
    def _(c):
        hop_copy(3, c).wait_recv()
        multiply(A, stream.at[3], c)

    hand_out(A, 1 - core)
    pass_on(A)

    def arrived(direction, role, place):
        ref = ends.at[direction, role, place]
        remote(ref, ref, end_send.at[A, 0], end_recv.at[direction, role, place], k, sibling).wait_recv()

    arrived(2, 0, 1 - core)
    arrived(2, 1, 0)
    arrived(2, 1, 1)
    arrived(1, 0, 1)
    arrived(1, 1, 1)

    @pl.when(core != level // 3)
    def _():
        arrived(1, 0, 0)

    @pl.when(core != (level + 2) // 3)
    def _():
        arrived(1, 1, 0)

    arrived(0, 1 - core, 0)
    arrived(0, 0, 1)
    arrived(0, 1, 1)

    z_real = jnp.zeros((16, NB), jnp.float32)
    z_imag = jnp.zeros((16, NB), jnp.float32)
    own_column = (
        lax.broadcasted_iota(jnp.int32, (16, NB), 0) + p * 16 == lax.broadcasted_iota(jnp.int32, (16, NB), 1)
    )
    for direction in range(3):
        ahead = ends[direction, 0, 0] + ends[direction, 0, 1]
        behind = ends[direction, 1, 0] + ends[direction, 1, 1]
        real, imag = ahead[0:16], ahead[16:32]
        diag_real, diag_imag = ahead[32:33], ahead[36:37]
        corr_out[direction, 0] = real
        corr_out[direction, 1] = imag
        back_real, back_imag = behind[0:16], behind[16:32]
        row_real = jnp.sum(jnp.where(own_column, back_real, 0.0), axis=1, keepdims=True)
        row_imag = jnp.sum(jnp.where(own_column, back_imag, 0.0), axis=1, keepdims=True)
        scale = weight[direction]
        z_real += scale * (
            real * diag_real + imag * diag_imag - (back_real * row_real + back_imag * row_imag)
        )
        z_imag += scale * (
            imag * diag_real - real * diag_imag - (back_imag * row_real - back_real * row_imag)
        )
    zrows[p, 0:16, :] = z_real
    zrows[p, 16:32, :] = z_imag

    def z_copy(j):
        dest = (q + j) % NQ * 2 + core
        return remote(zrows.at[p], zrows.at[p], z_send.at[j], z_recv.at[j], k, dest)

    def z_share(j):
        owner = (q + NQ - j) % NQ * 2 + core
        return remote(zrows.at[owner], zrows.at[owner], zz_send.at[j], zz_recv.at[j], k, sibling)

    @pl.loop(1, NQ)
    def _(j):
        z_copy(j).start()

    z_share(0).start()

    @pl.loop(1, NQ)
    def _(j):
        owner = (q + NQ - j) % NQ * 2 + core
        remote(zrows.at[owner], zrows.at[owner], z_send.at[j], z_recv.at[j], k, sibling).wait_recv()
        z_share(j).start()

    @pl.loop(0, NQ)
    def _(j):
        owner = (q + NQ - j) % NQ * 2 + 1 - core
        remote(zrows.at[owner], zrows.at[owner], zz_send.at[j], zz_recv.at[j], k, sibling).wait_recv()

    real = zrows[:, 0:16, :].reshape(NB, NB)
    imag = zrows[:, 16:32, :].reshape(NB, NB)
    grad_out[0] = 0.5 * (real - real.T)
    grad_out[1] = 0.5 * (imag + imag.T)

    list_copy(0).wait_send()
    list_copy(1).wait_send()
    other_copy.wait_send()

    @pl.loop(0, CHUNKS)
    def _(c):
        own_copy(c).wait_send()
        for h in range(1, HOPS):
            hop_copy(h, c).wait_send()

    def sent(slot):
        @pl.loop(1, NQ)
        def _(j):
            part_copy(slot, j).wait_send()

        for copy in end_copies(slot)[1]:
            copy.wait_send()

    sent(A)
    sent(C)

    @pl.when(b_here)
    def _():
        sent(B)

    @pl.when(w_here)
    def _():
        sent(W)

    z_share(0).wait_send()

    @pl.loop(1, NQ)
    def _(j):
        z_copy(j).wait_send()
        z_share(j).wait_send()


def local(wave, wave_perm, shell_weight):
    dma = pltpu.SemaphoreType.DMA
    vmem = pl.BlockSpec(memory_space=pltpu.VMEM)
    correlation, gradient = pl.pallas_call(
        kernel,
        out_shape=(
            jax.ShapeDtypeStruct((3, 2, 16, NB), jnp.float32),
            jax.ShapeDtypeStruct((2, NB, NB), jnp.float32),
        ),
        in_specs=[vmem, vmem, pl.BlockSpec(memory_space=pltpu.SMEM)],
        out_specs=(vmem, vmem),
        scratch_shapes=[
            pltpu.VMEM((HOPS, 2, NB, NG), jnp.bfloat16),
            pltpu.VMEM((2, NB, NG), jnp.bfloat16),
            pltpu.VMEM((4, 2 * NB, NG), jnp.bfloat16),
            pltpu.VMEM((2, NB, NB), jnp.float32),
            pltpu.VMEM((3, 3, 1, NG), jnp.int32),
            pltpu.VMEM((4, NQ, BLOCK, NB), jnp.float32),
            pltpu.VMEM((4, NQ, BLOCK, NB), jnp.float32),
            pltpu.VMEM((4, 2, HALF, NB), jnp.float32),
            pltpu.VMEM((3, 2, 2, HALF, NB), jnp.float32),
            pltpu.VMEM((2 * NQ, 32, NB), jnp.float32),
            dma((HOPS, CHUNKS)), dma((HOPS, CHUNKS)), dma, dma, dma((2,)), dma((2,)),
            dma((4, NQ)), dma((4, NQ)), dma((4, 3)), dma((3, 2, 2)),
            dma((NQ,)), dma((NQ,)), dma((NQ,)), dma((NQ,)),
        ],
        compiler_params=pltpu.CompilerParams(
            collective_id=0, has_side_effects=True, vmem_limit_bytes=48 * 1024 * 1024
        ),
        cost_estimate=pl.CostEstimate(
            flops=2 * 4 * 512 * NG * (NG + 512), bytes_accessed=4 * 512 * NG, transcendentals=0
        ),
    )(wave[0], wave_perm[0][:, None, :], shell_weight)
    return correlation[None], gradient[None]


def solution(mesh):
    placed = (P("ka", None, None, "pw"), P("ka", None, "pw"), P())
    return jax.shard_map(
        local,
        mesh=mesh,
        in_specs=placed,
        out_specs=(P("ka", None, None, "pw", None), P("ka", None, None, None)),
        check_vma=False,
    )
```

```python
import jax
import jax.numpy as jnp
from jax import lax
from jax.experimental import pallas as pl
from jax.experimental.pallas import tpu as pltpu
from jax.sharding import PartitionSpec as P

MESH = pl.DeviceIdType.MESH
NK = 32
NB = 256
NG = 1280
NQ = 8
HOPS = 4
CHUNKS = 4
ROWS = NB // CHUNKS
BLOCKS = ROWS // 16
A, B, W, C = range(4)
BLOCK = 72
HALF = 40


def kernel(
    wave_in, wave_halves, perm, weight, corr_out, grad_out,
    wave, stream, other, turned, product, lists, part, gathered, reduced, ends, zrows,
    stream_send, stream_recv, other_send, other_recv, list_send, list_recv,
    part_send, part_recv, end_send, end_recv, z_send, z_recv, zz_send, zz_recv, wave_sem, list_sem,
):
    k = lax.axis_index("ka")
    p = lax.axis_index("pw")
    core = p % 2
    q = p // 2
    sibling = p + 1 - 2 * core
    level = k // 2 % 4
    group = k // 8 * 8
    inner = k % 8
    to_next = (k + 30 + 4 * core) % NK
    a_up, a_down = (k + 8) % NK, (k + 24) % NK
    b_up, b_down = group + (inner + 2) % 8, group + (inner + 6) % 8
    flip = k + 1 - 2 * (k % 2)
    a_end = (k + 8 + 16 * core) % NK
    b_end = group + (inner + 2 + 4 * core) % 8
    w_end = group + (inner + 6 - 4 * core) % 8
    b_here = level != 3 - 3 * core
    w_here = level == 3 * core

    def remote(src, dst, send_sem, recv_sem, ka, pw):
        return pltpu.make_async_remote_copy(
            src_ref=src, dst_ref=dst, send_sem=send_sem, recv_sem=recv_sem,
            device_id=(ka, pw), device_id_type=MESH,
        )

    wave_copy = pltpu.make_async_copy(wave_in, wave, wave_sem)
    own_list_copy = pltpu.make_async_copy(perm, lists.at[0], list_sem)
    wave_copy.start()
    own_list_copy.start()

    barrier = pltpu.get_barrier_semaphore()
    peers = [((k + 2) % NK, p), ((k + 30) % NK, p), (k, sibling)]
    for end in (a_up, a_down, b_up, b_down, flip):
        peers += [(end, 2 * q), (end, 2 * q + 1)]
    peers += [(k, (q + j) % NQ * 2 + core) for j in range(1, NQ)]
    for peer in peers:
        pl.semaphore_signal(barrier, inc=1, device_id=peer, device_id_type=MESH)
    pl.semaphore_wait(barrier, len(peers))

    def blocks(c):
        return pl.ds(c * BLOCKS, BLOCKS)

    def own_copy(c, source):
        return remote(
            source, stream.at[0, :, blocks(c)],
            stream_send.at[0, c], stream_recv.at[0, c], to_next, p,
        )

    def hop_copy(h, c):
        return remote(
            stream.at[h - 1, :, blocks(c)], stream.at[h, :, blocks(c)],
            stream_send.at[h, c], stream_recv.at[h, c], to_next, p,
        )

    def list_copy(i):
        return remote(
            perm.at[i], lists.at[i + 1, i], list_send.at[i], list_recv.at[i], (a_up, b_up)[i], p
        )

    other_copy = remote(wave_in, other, other_send, other_recv, flip, p)

    list_copy(0).start()
    list_copy(1).start()

    @pl.when(core == 0)
    def _():
        for c in range(CHUNKS):
            own_copy(c, wave_in.at[:, blocks(c)]).start()

    @pl.when(core == 1)
    def _():
        for c in range(CHUNKS):
            own_copy(c, wave_halves.at[:, c % 2 * 4:c % 2 * 4 + 4, c // 2]).start()

    other_copy.start()
    own_list_copy.wait()
    wave_copy.wait()
    list_copy(0).wait_recv()
    list_copy(1).wait_recv()

    def turn(slot):
        which = (1 - core) * 2 * (slot // 2) * (1 - slot % 2) + core * ((slot + 1) % 3) * (1 - slot // 2)
        direction = (slot + 1) // 2
        at_start = (1 - core) * (1 - slot // 2 * (1 - slot % 2)) + core * (slot // 2)

        @pl.when(at_start == 1)
        def _():
            @pl.loop(0, NG // 256)
            def _(j):
                row = lists[which, direction] - p * NG
                wanted = lax.broadcasted_iota(jnp.int32, (256, NG), 0) + j * 256
                pick = jnp.where(wanted == row, 1.0, 0.0).astype(jnp.bfloat16)
                value = lax.dot_general(
                    wave[...].reshape(2 * NB, NG), pick, (((1,), (1,)), ((), ())),
                    preferred_element_type=jnp.float32,
                )
                turned[slot, :, pl.ds(pl.multiple_of(j * 256, 256), 256)] = value.astype(jnp.bfloat16)

        @pl.when(at_start == 0)
        def _():
            @pl.loop(0, NG // 256)
            def _(j):
                columns = pl.ds(pl.multiple_of(j * 256, 256), 256)
                row = lists[which, direction, :, columns] - p * NG
                held = lax.broadcasted_iota(jnp.int32, (NG, 256), 0)
                pick = jnp.where(held == row, 1.0, 0.0).astype(jnp.bfloat16)
                value = lax.dot_general(
                    wave[...].reshape(2 * NB, NG), pick, (((1,), (0,)), ((), ())),
                    preferred_element_type=jnp.float32,
                )
                turned[slot, :, columns] = value.astype(jnp.bfloat16)

    def multiply(slot, source, c, order):
        value = lax.dot_general(
            source[:, blocks(c)].reshape(2 * ROWS, NG), turned[slot], (((1,), (1,)), ((), ())),
            preferred_element_type=jnp.float32,
        )
        real = value[:ROWS, :NB] + value[ROWS:, NB:]
        imag = value[:ROWS, NB:] - value[ROWS:, :NB]
        for i in range(BLOCKS):
            n = c * BLOCKS + i
            block = n + order * (n % NQ * 2 + n // NQ - n)
            rows = pl.ds(pl.multiple_of(block * 16, 16), 16)
            product[0, rows, :] = real[16 * i:16 * i + 16]
            product[1, rows, :] = imag[16 * i:16 * i + 16]

    def part_copy(slot, j):
        dest = (q + j) % NQ
        return remote(
            part.at[slot, dest], gathered.at[slot, j],
            part_send.at[slot, j], part_recv.at[slot, j], k, dest * 2 + core,
        )

    def hand_out(slot, at_start):
        swap = jnp.broadcast_to(at_start, (NB, NB)) > 0
        real, imag = product[0], product[1]
        real = jnp.where(swap, real.T, real)
        imag = jnp.where(swap, -imag.T, imag)
        eye = lax.broadcasted_iota(jnp.int32, (NB, NB), 0) == lax.broadcasted_iota(jnp.int32, (NB, NB), 1)
        diag_real = jnp.sum(jnp.where(eye, real, 0.0), axis=0, keepdims=True)
        diag_imag = jnp.sum(jnp.where(eye, imag, 0.0), axis=0, keepdims=True)
        first = lax.broadcasted_iota(jnp.int32, (8, NB), 0) < 4
        diag = jnp.where(first, diag_real, diag_imag)
        real = real.reshape(NQ, 2, 16, NB)
        imag = imag.reshape(NQ, 2, 16, NB)
        part[slot, :, 0:16, :] = real[:, 0]
        part[slot, :, 16:32, :] = imag[:, 0]
        part[slot, :, 32:48, :] = real[:, 1]
        part[slot, :, 48:64, :] = imag[:, 1]
        part[slot, :, 64:72, :] = jnp.broadcast_to(diag[None], (NQ, 8, NB))

        @pl.loop(1, NQ)
        def _(j):
            part_copy(slot, j).start()

    def end_copies(slot):
        if slot == C:
            direction, role, far_role, end, near, far = 2, 0, 1, flip, core, core
        elif slot == W:
            direction, role, far_role, end, near, far = 1, 1 - core, core, w_end, 0, 1
        else:
            direction, role, far_role, end, near, far = 1, core, 1 - core, b_end, 0, 1
        local = (direction, role, near)
        target = ends.at[direction, far_role, far]
        sem = end_recv.at[direction, far_role, far]
        copies = [
            remote(
                reduced.at[slot, 1 - core], ends.at[direction, role, near],
                end_send.at[slot, 0], end_recv.at[direction, role, near], k, sibling,
            ),
            remote(reduced.at[slot, 0], target, end_send.at[slot, 1], sem, end, 2 * q),
            remote(reduced.at[slot, 1], target, end_send.at[slot, 2], sem, end, 2 * q + 1),
        ]
        return local, copies

    def pass_on(slot):
        @pl.loop(1, NQ)
        def _(j):
            part_copy(slot, j).wait_recv()

        total = part[slot, q]
        for j in range(1, NQ):
            total = total + gathered[slot, j]
        reduced[slot, 0, 0:32, :] = total[0:32]
        reduced[slot, 0, 32:40, :] = total[64:72]
        reduced[slot, 1, 0:32, :] = total[32:64]
        reduced[slot, 1, 32:40, :] = total[64:72]
        local, copies = end_copies(slot)
        for copy in copies:
            copy.start()
        ends[local[0], local[1], local[2]] = reduced[slot, core]

    def a_piece(ref, on, h):
        if on == 0:
            return ref.at[:, 128 * h:128 * h + 128]
        return ref.at[32 * h:(32, BLOCK)[h], :]

    def a_part_copy(on, h, j):
        dest = (q + j) % NQ
        row = (4, A)[h]
        return remote(
            a_piece(part.at[A, dest], on, h), a_piece(gathered.at[A, j], on, h),
            part_send.at[row, j], part_recv.at[row, j], k, dest * 2 + core,
        )

    def a_diag(real, imag, h):
        shape = real.shape
        eye = (
            lax.broadcasted_iota(jnp.int32, shape, 0) == lax.broadcasted_iota(jnp.int32, shape, 1) + 128 * h
        )
        diag_real = jnp.sum(jnp.where(eye, real, 0.0), axis=0, keepdims=True)
        diag_imag = jnp.sum(jnp.where(eye, imag, 0.0), axis=0, keepdims=True)
        first = lax.broadcasted_iota(jnp.int32, (8, shape[1]), 0) < 4
        return jnp.broadcast_to(jnp.where(first, diag_real, diag_imag)[None], (NQ, 8, shape[1]))

    def a_hand_out(h):
        @pl.when(core == 0)
        def _():
            columns = slice(128 * h, 128 * h + 128)
            real = product[0, columns, :].T
            imag = -product[1, columns, :].T
            part[A, :, 64:72, columns] = a_diag(real, imag, h)
            real = real.reshape(NQ, 2, 16, 128)
            imag = imag.reshape(NQ, 2, 16, 128)
            for i in range(2):
                part[A, :, 32 * i:32 * i + 16, columns] = real[:, i]
                part[A, :, 32 * i + 16:32 * i + 32, columns] = imag[:, i]

            @pl.loop(1, NQ)
            def _(j):
                a_part_copy(0, h, j).start()

        @pl.when(core == 1)
        def _():
            real, imag = product[0], product[1]
            if h == 1:
                part[A, :, 64:72, :] = a_diag(real, imag, 0)
            part[A, :, 32 * h:32 * h + 16, :] = real.reshape(NQ, 2, 16, NB)[:, h]
            part[A, :, 32 * h + 16:32 * h + 32, :] = imag.reshape(NQ, 2, 16, NB)[:, h]

            @pl.loop(1, NQ)
            def _(j):
                a_part_copy(1, h, j).start()

    def a_end_copies(on, h):
        near, near_sem = ends.at[0, on, 0], end_recv.at[0, on, 0]
        far, far_sem = ends.at[0, 1 - on, 1], end_recv.at[0, 1 - on, 1]
        row = (4, A)[h]
        if on == 0:
            rows, columns = slice(0, HALF), slice(128 * h, 128 * h + 128)
            last = [(1, near, near_sem, k, sibling), (1, far, far_sem, a_end, 2 * q + 1)]
            todo = last + [(0, far, far_sem, a_end, 2 * q)]
            cuts = [(rows, columns)] * 3
        else:
            rows, columns = slice(32 * h, (32, HALF)[h]), slice(0, NB)
            todo = [(0, near, near_sem, k, sibling), (0, far, far_sem, a_end, 2 * q)]
            cuts = [(rows, columns)] * 2
            if h == 1:
                todo = todo + [(1, far, far_sem, a_end, 2 * q + 1)]
                cuts = cuts + [(slice(0, HALF), columns)]
        return [
            remote(
                reduced.at[A, half, cut[0], cut[1]], target.at[cut[0], cut[1]],
                end_send.at[row, i], sem, ka, pw,
            )
            for i, ((half, target, sem, ka, pw), cut) in enumerate(zip(todo, cuts))
        ]

    def a_pass_on(h):
        for on in range(2):
            @pl.when(core == on)
            def _():
                @pl.loop(1, NQ)
                def _(j):
                    a_part_copy(on, h, j).wait_recv()

                total = a_piece(part.at[A, q], on, h)[...]
                for j in range(1, NQ):
                    total = total + a_piece(gathered.at[A, j], on, h)[...]
                if on == 0:
                    columns = slice(128 * h, 128 * h + 128)
                    for half in range(2):
                        reduced[A, half, 0:32, columns] = total[32 * half:32 * half + 32]
                        reduced[A, half, 32:40, columns] = total[64:72]
                else:
                    reduced[A, h, 0:32, :] = total[0:32]
                    if h == 1:
                        reduced[A, 0, 32:40, :] = total[32:40]
                        reduced[A, 1, 32:40, :] = total[32:40]
                for copy in a_end_copies(on, h):
                    copy.start()

        if h == 1:
            ends[0, core, 0] = reduced[A, core]

    @pl.loop(0, CHUNKS)
    def _(c):
        turn(3 - c)
        own_copy(c, stream.at[0, :, blocks(c)]).wait_recv()
        hop_copy(1, c).start()

    @pl.when(b_here)
    def _():
        @pl.loop(0, CHUNKS)
        def _(c):
            multiply(B, stream.at[0], c, core)

        hand_out(B, 1 - core)

    @pl.loop(0, CHUNKS)
    def _(c):
        hop_copy(1, c).wait_recv()
        hop_copy(2, c).start()

    other_copy.wait_recv()

    @pl.loop(0, CHUNKS)
    def _(c):
        multiply(C, other, c, 0)

    hand_out(C, 1)

    @pl.loop(0, CHUNKS)
    def _(c):
        hop_copy(2, c).wait_recv()
        hop_copy(3, c).start()

    @pl.when(w_here)
    def _():
        @pl.loop(0, CHUNKS)
        def _(c):
            multiply(W, stream.at[2], c, core)

        hand_out(W, core)

    @pl.when(b_here)
    def _():
        pass_on(B)

    pass_on(C)

    @pl.loop(0, CHUNKS // 2)
    def _(c):
        hop_copy(3, c).wait_recv()
        multiply(A, stream.at[3], c, core)

    a_hand_out(0)

    @pl.when(w_here)
    def _():
        pass_on(W)

    @pl.loop(CHUNKS // 2, CHUNKS)
    def _(c):
        hop_copy(3, c).wait_recv()
        multiply(A, stream.at[3], c, core)

    a_hand_out(1)
    a_pass_on(0)
    a_pass_on(1)

    def arrived(direction, role, place):
        ref = ends.at[direction, role, place]
        remote(ref, ref, end_send.at[A, 0], end_recv.at[direction, role, place], k, sibling).wait_recv()

    arrived(2, 0, 1 - core)
    arrived(2, 1, 0)
    arrived(2, 1, 1)
    arrived(1, 0, 1)
    arrived(1, 1, 1)

    @pl.when(core != level // 3)
    def _():
        arrived(1, 0, 0)

    @pl.when(core != (level + 2) // 3)
    def _():
        arrived(1, 1, 0)

    arrived(0, 1 - core, 0)
    arrived(0, 0, 1)
    arrived(0, 1, 1)

    z_real = jnp.zeros((16, NB), jnp.float32)
    z_imag = jnp.zeros((16, NB), jnp.float32)
    own_column = (
        lax.broadcasted_iota(jnp.int32, (16, NB), 0) + p * 16 == lax.broadcasted_iota(jnp.int32, (16, NB), 1)
    )
    for direction in range(3):
        ahead = ends[direction, 0, 0] + ends[direction, 0, 1]
        behind = ends[direction, 1, 0] + ends[direction, 1, 1]
        real, imag = ahead[0:16], ahead[16:32]
        diag_real, diag_imag = ahead[32:33], ahead[36:37]
        corr_out[direction, 0] = real
        corr_out[direction, 1] = imag
        back_real, back_imag = behind[0:16], behind[16:32]
        row_real = jnp.sum(jnp.where(own_column, back_real, 0.0), axis=1, keepdims=True)
        row_imag = jnp.sum(jnp.where(own_column, back_imag, 0.0), axis=1, keepdims=True)
        scale = weight[direction]
        z_real += scale * (
            real * diag_real + imag * diag_imag - (back_real * row_real + back_imag * row_imag)
        )
        z_imag += scale * (
            imag * diag_real - real * diag_imag - (back_imag * row_real - back_real * row_imag)
        )
    zrows[p, 0:16, :] = z_real
    zrows[p, 16:32, :] = z_imag

    def z_copy(j):
        dest = (q + j) % NQ * 2 + core
        return remote(zrows.at[p], zrows.at[p], z_send.at[j], z_recv.at[j], k, dest)

    def z_share(j):
        owner = (q + NQ - j) % NQ * 2 + core
        return remote(zrows.at[owner], zrows.at[owner], zz_send.at[j], zz_recv.at[j], k, sibling)

    @pl.loop(1, NQ)
    def _(j):
        z_copy(j).start()

    z_share(0).start()

    @pl.loop(1, NQ)
    def _(j):
        owner = (q + NQ - j) % NQ * 2 + core
        remote(zrows.at[owner], zrows.at[owner], z_send.at[j], z_recv.at[j], k, sibling).wait_recv()
        z_share(j).start()

    @pl.loop(0, NQ)
    def _(j):
        owner = (q + NQ - j) % NQ * 2 + 1 - core
        remote(zrows.at[owner], zrows.at[owner], zz_send.at[j], zz_recv.at[j], k, sibling).wait_recv()

    real = zrows[:, 0:16, :].reshape(NB, NB)
    imag = zrows[:, 16:32, :].reshape(NB, NB)
    grad_out[0] = 0.5 * (real - real.T)
    grad_out[1] = 0.5 * (imag + imag.T)

    list_copy(0).wait_send()
    list_copy(1).wait_send()
    other_copy.wait_send()

    @pl.loop(0, CHUNKS)
    def _(c):
        own_copy(c, stream.at[0, :, blocks(c)]).wait_send()
        for h in range(1, HOPS):
            hop_copy(h, c).wait_send()

    def sent(slot):
        @pl.loop(1, NQ)
        def _(j):
            part_copy(slot, j).wait_send()

        for copy in end_copies(slot)[1]:
            copy.wait_send()

    for on in range(2):
        @pl.when(core == on)
        def _():
            for h in range(2):
                @pl.loop(1, NQ)
                def _(j):
                    a_part_copy(on, h, j).wait_send()

                for copy in a_end_copies(on, h):
                    copy.wait_send()

    sent(C)

    @pl.when(b_here)
    def _():
        sent(B)

    @pl.when(w_here)
    def _():
        sent(W)

    z_share(0).wait_send()

    @pl.loop(1, NQ)
    def _(j):
        z_copy(j).wait_send()
        z_share(j).wait_send()


def local(wave, wave_perm, shell_weight):
    dma = pltpu.SemaphoreType.DMA
    vmem = pl.BlockSpec(memory_space=pltpu.VMEM)
    correlation, gradient = pl.pallas_call(
        kernel,
        out_shape=(
            jax.ShapeDtypeStruct((3, 2, 16, NB), jnp.float32),
            jax.ShapeDtypeStruct((2, NB, NB), jnp.float32),
        ),
        in_specs=[pl.BlockSpec(memory_space=pl.ANY)] * 3 + [pl.BlockSpec(memory_space=pltpu.SMEM)],
        out_specs=(vmem, vmem),
        scratch_shapes=[
            pltpu.VMEM((2, 16, 16, NG), jnp.bfloat16),
            pltpu.VMEM((HOPS, 2, 16, 16, NG), jnp.bfloat16),
            pltpu.VMEM((2, 16, 16, NG), jnp.bfloat16),
            pltpu.VMEM((4, 2 * NB, NG), jnp.bfloat16),
            pltpu.VMEM((2, NB, NB), jnp.float32),
            pltpu.VMEM((3, 3, 1, NG), jnp.int32),
            pltpu.VMEM((4, NQ, BLOCK, NB), jnp.float32),
            pltpu.VMEM((4, NQ, BLOCK, NB), jnp.float32),
            pltpu.VMEM((4, 2, HALF, NB), jnp.float32),
            pltpu.VMEM((3, 2, 2, HALF, NB), jnp.float32),
            pltpu.VMEM((2 * NQ, 32, NB), jnp.float32),
            dma((HOPS, CHUNKS)), dma((HOPS, CHUNKS)), dma, dma, dma((2,)), dma((2,)),
            dma((5, NQ)), dma((5, NQ)), dma((5, 3)), dma((3, 2, 2)),
            dma((NQ,)), dma((NQ,)), dma((NQ,)), dma((NQ,)), dma, dma,
        ],
        compiler_params=pltpu.CompilerParams(
            collective_id=0, has_side_effects=True, vmem_limit_bytes=48 * 1024 * 1024
        ),
        cost_estimate=pl.CostEstimate(
            flops=2 * 4 * 512 * NG * (NG + 512), bytes_accessed=4 * 512 * NG, transcendentals=0
        ),
    )(
        pltpu.with_memory_space_constraint(wave.reshape(2, 16, 16, NG), pltpu.HBM),
        pltpu.with_memory_space_constraint(wave.reshape(2, NQ, 2, 16, NG), pltpu.HBM),
        pltpu.with_memory_space_constraint(wave_perm[0][:, None, :], pltpu.HBM),
        pltpu.with_memory_space_constraint(shell_weight, pltpu.HBM),
    )
    return correlation[None], gradient[None]


def solution(mesh):
    placed = (P("ka", None, None, "pw"), P("ka", None, "pw"), P())
    return jax.shard_map(
        local,
        mesh=mesh,
        in_specs=placed,
        out_specs=(P("ka", None, None, "pw", None), P("ka", None, None, None)),
        check_vma=False,
    )
```

```python
import jax
import jax.numpy as jnp
from jax import lax
from jax.experimental import pallas as pl
from jax.experimental.pallas import tpu as pltpu
from jax.sharding import PartitionSpec as P

MESH = pl.DeviceIdType.MESH
NK = 32
NB = 256
NG = 1280
NQ = 8
HOPS = 4
CHUNKS = 4
ROWS = NB // CHUNKS
BLOCKS = ROWS // 16
A, B, W, C = range(4)
BLOCK = 72
HALF = 40


def kernel(
    wave_in, wave_halves, perm, weight, corr_out, grad_out,
    wave, stream, other, turned, product, lists, part, gathered, reduced, ends, zrows,
    stream_send, stream_recv, other_send, other_recv, list_send, list_recv,
    part_send, part_recv, end_send, end_recv, z_send, z_recv, zz_send, zz_recv, wave_sem, list_sem, told,
):
    k = lax.axis_index("ka")
    p = lax.axis_index("pw")
    core = p % 2
    q = p // 2
    sibling = p + 1 - 2 * core
    level = k // 2 % 4
    group = k // 8 * 8
    inner = k % 8
    to_next = (k + 30 + 4 * core) % NK
    a_up, a_down = (k + 8) % NK, (k + 24) % NK
    b_up, b_down = group + (inner + 2) % 8, group + (inner + 6) % 8
    flip = k + 1 - 2 * (k % 2)
    a_end = (k + 8 + 16 * core) % NK
    b_end = group + (inner + 2 + 4 * core) % 8
    w_end = group + (inner + 6 - 4 * core) % 8
    b_here = level != 3 - 3 * core
    w_here = level == 3 * core

    def remote(src, dst, send_sem, recv_sem, ka, pw):
        return pltpu.make_async_remote_copy(
            src_ref=src, dst_ref=dst, send_sem=send_sem, recv_sem=recv_sem,
            device_id=(ka, pw), device_id_type=MESH,
        )

    wave_copy = pltpu.make_async_copy(wave_in, wave, wave_sem)
    own_list_copy = pltpu.make_async_copy(perm, lists.at[0], list_sem)
    wave_copy.start()
    own_list_copy.start()

    around = [
        ((k + 2) % NK, p), ((k + 30) % NK, p), (flip, p), (flip, (q + 4) % NQ * 2 + core),
        (k, (q // 4 * 4 + (q + 1) % 4) * 2 + core), (k, (q // 4 * 4 + (q + 3) % 4) * 2 + core), (k, sibling),
    ]

    def tell(sem):
        for neighbour in around:
            pl.semaphore_signal(sem, inc=1, device_id=neighbour, device_id_type=MESH)

    barrier = pltpu.get_barrier_semaphore()
    tell(barrier)
    pl.semaphore_wait(barrier, len(around))

    def blocks(c):
        return pl.ds(c * BLOCKS, BLOCKS)

    def own_copy(c, source):
        return remote(
            source, stream.at[0, :, blocks(c)],
            stream_send.at[0, c], stream_recv.at[0, c], to_next, p,
        )

    def hop_copy(h, c):
        return remote(
            stream.at[h - 1, :, blocks(c)], stream.at[h, :, blocks(c)],
            stream_send.at[h, c], stream_recv.at[h, c], to_next, p,
        )

    def list_copy(h):
        source = perm if h == 0 else lists.at[h]
        return remote(
            source.at[0:2], lists.at[h + 1, 0:2], list_send.at[h], list_recv.at[h], to_next, p
        )

    other_copy = remote(wave_in, other, other_send, other_recv, flip, p)

    list_copy(0).start()

    @pl.when(core == 0)
    def _():
        for c in range(CHUNKS):
            own_copy(c, wave_in.at[:, blocks(c)]).start()

    @pl.when(core == 1)
    def _():
        for c in range(CHUNKS):
            own_copy(c, wave_halves.at[:, c % 2 * 4:c % 2 * 4 + 4, c // 2]).start()

    other_copy.start()
    tell(told.at[0])
    own_list_copy.wait()
    wave_copy.wait()

    def turn(slot):
        which = (1 - core) * 3 * (slot // 2) * (1 - slot % 2) + core * (4 - 3 * slot) * (1 - slot // 2)
        direction = (slot + 1) // 2
        at_start = (1 - core) * (1 - slot // 2 * (1 - slot % 2)) + core * (slot // 2)

        @pl.when(at_start == 1)
        def _():
            @pl.loop(0, NG // 256)
            def _(j):
                row = lists[which, direction] - p * NG
                wanted = lax.broadcasted_iota(jnp.int32, (256, NG), 0) + j * 256
                pick = jnp.where(wanted == row, 1.0, 0.0).astype(jnp.bfloat16)
                value = lax.dot_general(
                    wave[...].reshape(2 * NB, NG), pick, (((1,), (1,)), ((), ())),
                    preferred_element_type=jnp.float32,
                )
                turned[slot, :, pl.ds(pl.multiple_of(j * 256, 256), 256)] = value.astype(jnp.bfloat16)

        @pl.when(at_start == 0)
        def _():
            @pl.loop(0, NG // 256)
            def _(j):
                columns = pl.ds(pl.multiple_of(j * 256, 256), 256)
                row = lists[which, direction, :, columns] - p * NG
                held = lax.broadcasted_iota(jnp.int32, (NG, 256), 0)
                pick = jnp.where(held == row, 1.0, 0.0).astype(jnp.bfloat16)
                value = lax.dot_general(
                    wave[...].reshape(2 * NB, NG), pick, (((1,), (0,)), ((), ())),
                    preferred_element_type=jnp.float32,
                )
                turned[slot, :, columns] = value.astype(jnp.bfloat16)

    def multiply(slot, source, c, order):
        value = lax.dot_general(
            source[:, blocks(c)].reshape(2 * ROWS, NG), turned[slot], (((1,), (1,)), ((), ())),
            preferred_element_type=jnp.float32,
        )
        real = value[:ROWS, :NB] + value[ROWS:, NB:]
        imag = value[:ROWS, NB:] - value[ROWS:, :NB]
        for i in range(BLOCKS):
            n = c * BLOCKS + i
            block = n + order * (n % NQ * 2 + n // NQ - n)
            rows = pl.ds(pl.multiple_of(block * 16, 16), 16)
            product[0, rows, :] = real[16 * i:16 * i + 16]
            product[1, rows, :] = imag[16 * i:16 * i + 16]

    def part_copy(slot, j):
        dest = (q + j) % NQ
        return remote(
            part.at[slot, dest], gathered.at[slot, j],
            part_send.at[slot, j], part_recv.at[slot, j], k, dest * 2 + core,
        )

    def hand_out(slot, at_start):
        swap = jnp.broadcast_to(at_start, (NB, NB)) > 0
        real, imag = product[0], product[1]
        real = jnp.where(swap, real.T, real)
        imag = jnp.where(swap, -imag.T, imag)
        eye = lax.broadcasted_iota(jnp.int32, (NB, NB), 0) == lax.broadcasted_iota(jnp.int32, (NB, NB), 1)
        diag_real = jnp.sum(jnp.where(eye, real, 0.0), axis=0, keepdims=True)
        diag_imag = jnp.sum(jnp.where(eye, imag, 0.0), axis=0, keepdims=True)
        first = lax.broadcasted_iota(jnp.int32, (8, NB), 0) < 4
        diag = jnp.where(first, diag_real, diag_imag)
        real = real.reshape(NQ, 2, 16, NB)
        imag = imag.reshape(NQ, 2, 16, NB)
        part[slot, :, 0:16, :] = real[:, 0]
        part[slot, :, 16:32, :] = imag[:, 0]
        part[slot, :, 32:48, :] = real[:, 1]
        part[slot, :, 48:64, :] = imag[:, 1]
        part[slot, :, 64:72, :] = jnp.broadcast_to(diag[None], (NQ, 8, NB))

        @pl.loop(1, NQ)
        def _(j):
            part_copy(slot, j).start()

    def end_copies(slot):
        if slot == C:
            direction, role, far_role, end, near, far = 2, 0, 1, flip, core, core
        elif slot == W:
            direction, role, far_role, end, near, far = 1, 1 - core, core, w_end, 0, 1
        else:
            direction, role, far_role, end, near, far = 1, core, 1 - core, b_end, 0, 1
        local = (direction, role, near)
        target = ends.at[direction, far_role, far]
        sem = end_recv.at[direction, far_role, far]
        copies = [
            remote(
                reduced.at[slot, 1 - core], ends.at[direction, role, near],
                end_send.at[slot, 0], end_recv.at[direction, role, near], k, sibling,
            ),
            remote(reduced.at[slot, 0], target, end_send.at[slot, 1], sem, end, 2 * q),
            remote(reduced.at[slot, 1], target, end_send.at[slot, 2], sem, end, 2 * q + 1),
        ]
        return local, copies

    def pass_on(slot):
        @pl.loop(1, NQ)
        def _(j):
            part_copy(slot, j).wait_recv()

        total = part[slot, q]
        for j in range(1, NQ):
            total = total + gathered[slot, j]
        reduced[slot, 0, 0:32, :] = total[0:32]
        reduced[slot, 0, 32:40, :] = total[64:72]
        reduced[slot, 1, 0:32, :] = total[32:64]
        reduced[slot, 1, 32:40, :] = total[64:72]
        local, copies = end_copies(slot)
        for copy in copies:
            copy.start()
        ends[local[0], local[1], local[2]] = reduced[slot, core]

    def a_piece(ref, on, h):
        if on == 0:
            return ref.at[:, 128 * h:128 * h + 128]
        return ref.at[32 * h:(32, BLOCK)[h], :]

    def a_part_copy(on, h, j):
        dest = (q + j) % NQ
        row = (4, A)[h]
        return remote(
            a_piece(part.at[A, dest], on, h), a_piece(gathered.at[A, j], on, h),
            part_send.at[row, j], part_recv.at[row, j], k, dest * 2 + core,
        )

    def a_diag(real, imag, h):
        shape = real.shape
        eye = (
            lax.broadcasted_iota(jnp.int32, shape, 0) == lax.broadcasted_iota(jnp.int32, shape, 1) + 128 * h
        )
        diag_real = jnp.sum(jnp.where(eye, real, 0.0), axis=0, keepdims=True)
        diag_imag = jnp.sum(jnp.where(eye, imag, 0.0), axis=0, keepdims=True)
        first = lax.broadcasted_iota(jnp.int32, (8, shape[1]), 0) < 4
        return jnp.broadcast_to(jnp.where(first, diag_real, diag_imag)[None], (NQ, 8, shape[1]))

    def a_hand_out(h):
        @pl.when(core == 0)
        def _():
            columns = slice(128 * h, 128 * h + 128)
            real = product[0, columns, :].T
            imag = -product[1, columns, :].T
            part[A, :, 64:72, columns] = a_diag(real, imag, h)
            real = real.reshape(NQ, 2, 16, 128)
            imag = imag.reshape(NQ, 2, 16, 128)
            for i in range(2):
                part[A, :, 32 * i:32 * i + 16, columns] = real[:, i]
                part[A, :, 32 * i + 16:32 * i + 32, columns] = imag[:, i]

            @pl.loop(1, NQ)
            def _(j):
                a_part_copy(0, h, j).start()

        @pl.when(core == 1)
        def _():
            real, imag = product[0], product[1]
            if h == 1:
                part[A, :, 64:72, :] = a_diag(real, imag, 0)
            part[A, :, 32 * h:32 * h + 16, :] = real.reshape(NQ, 2, 16, NB)[:, h]
            part[A, :, 32 * h + 16:32 * h + 32, :] = imag.reshape(NQ, 2, 16, NB)[:, h]

            @pl.loop(1, NQ)
            def _(j):
                a_part_copy(1, h, j).start()

    def a_end_copies(on, h):
        near, near_sem = ends.at[0, on, 0], end_recv.at[0, on, 0]
        far, far_sem = ends.at[0, 1 - on, 1], end_recv.at[0, 1 - on, 1]
        row = (4, A)[h]
        if on == 0:
            rows, columns = slice(0, HALF), slice(128 * h, 128 * h + 128)
            last = [(1, near, near_sem, k, sibling), (1, far, far_sem, a_end, 2 * q + 1)]
            todo = last + [(0, far, far_sem, a_end, 2 * q)]
            cuts = [(rows, columns)] * 3
        else:
            rows, columns = slice(32 * h, (32, HALF)[h]), slice(0, NB)
            todo = [(0, near, near_sem, k, sibling), (0, far, far_sem, a_end, 2 * q)]
            cuts = [(rows, columns)] * 2
            if h == 1:
                todo = todo + [(1, far, far_sem, a_end, 2 * q + 1)]
                cuts = cuts + [(slice(0, HALF), columns)]
        return [
            remote(
                reduced.at[A, half, cut[0], cut[1]], target.at[cut[0], cut[1]],
                end_send.at[row, i], sem, ka, pw,
            )
            for i, ((half, target, sem, ka, pw), cut) in enumerate(zip(todo, cuts))
        ]

    def a_pass_on(h):
        for on in range(2):
            @pl.when(core == on)
            def _():
                @pl.loop(1, NQ)
                def _(j):
                    a_part_copy(on, h, j).wait_recv()

                total = a_piece(part.at[A, q], on, h)[...]
                for j in range(1, NQ):
                    total = total + a_piece(gathered.at[A, j], on, h)[...]
                if on == 0:
                    columns = slice(128 * h, 128 * h + 128)
                    for half in range(2):
                        reduced[A, half, 0:32, columns] = total[32 * half:32 * half + 32]
                        reduced[A, half, 32:40, columns] = total[64:72]
                else:
                    reduced[A, h, 0:32, :] = total[0:32]
                    if h == 1:
                        reduced[A, 0, 32:40, :] = total[32:40]
                        reduced[A, 1, 32:40, :] = total[32:40]
                for copy in a_end_copies(on, h):
                    copy.start()

        if h == 1:
            ends[0, core, 0] = reduced[A, core]

    turn(C)
    list_copy(0).wait_recv()
    list_copy(1).start()
    for c in range(CHUNKS):
        own_copy(c, stream.at[0, :, blocks(c)]).wait_recv()
        hop_copy(1, c).start()
        pl.semaphore_wait(told.at[c], len(around))
        if c < CHUNKS - 1:
            tell(told.at[c + 1])

    turn(B)

    @pl.when(b_here)
    def _():
        @pl.loop(0, CHUNKS)
        def _(c):
            multiply(B, stream.at[0], c, core)

        hand_out(B, 1 - core)

    list_copy(1).wait_recv()
    list_copy(2).start()

    @pl.loop(0, CHUNKS)
    def _(c):
        hop_copy(1, c).wait_recv()
        hop_copy(2, c).start()

    other_copy.wait_recv()

    @pl.loop(0, CHUNKS)
    def _(c):
        multiply(C, other, c, 0)

    hand_out(C, 1)

    list_copy(2).wait_recv()
    list_copy(3).start()
    @pl.loop(0, CHUNKS)
    def _(c):
        hop_copy(2, c).wait_recv()
        hop_copy(3, c).start()

    @pl.when(w_here)
    def _():
        turn(W)

        @pl.loop(0, CHUNKS)
        def _(c):
            multiply(W, stream.at[2], c, core)

        hand_out(W, core)

    @pl.when(b_here)
    def _():
        pass_on(B)

    pass_on(C)

    list_copy(3).wait_recv()
    turn(A)

    @pl.loop(0, CHUNKS // 2)
    def _(c):
        hop_copy(3, c).wait_recv()
        multiply(A, stream.at[3], c, core)

    a_hand_out(0)

    @pl.when(w_here)
    def _():
        pass_on(W)

    @pl.loop(CHUNKS // 2, CHUNKS)
    def _(c):
        hop_copy(3, c).wait_recv()
        multiply(A, stream.at[3], c, core)

    a_hand_out(1)
    a_pass_on(0)
    a_pass_on(1)

    def arrived(direction, role, place):
        ref = ends.at[direction, role, place]
        remote(ref, ref, end_send.at[A, 0], end_recv.at[direction, role, place], k, sibling).wait_recv()

    arrived(2, 0, 1 - core)
    arrived(2, 1, 0)
    arrived(2, 1, 1)
    arrived(1, 0, 1)
    arrived(1, 1, 1)

    @pl.when(core != level // 3)
    def _():
        arrived(1, 0, 0)

    @pl.when(core != (level + 2) // 3)
    def _():
        arrived(1, 1, 0)

    arrived(0, 1 - core, 0)
    arrived(0, 0, 1)
    arrived(0, 1, 1)

    z_real = jnp.zeros((16, NB), jnp.float32)
    z_imag = jnp.zeros((16, NB), jnp.float32)
    own_column = (
        lax.broadcasted_iota(jnp.int32, (16, NB), 0) + p * 16 == lax.broadcasted_iota(jnp.int32, (16, NB), 1)
    )
    for direction in range(3):
        ahead = ends[direction, 0, 0] + ends[direction, 0, 1]
        behind = ends[direction, 1, 0] + ends[direction, 1, 1]
        real, imag = ahead[0:16], ahead[16:32]
        diag_real, diag_imag = ahead[32:33], ahead[36:37]
        corr_out[direction, 0] = real
        corr_out[direction, 1] = imag
        back_real, back_imag = behind[0:16], behind[16:32]
        row_real = jnp.sum(jnp.where(own_column, back_real, 0.0), axis=1, keepdims=True)
        row_imag = jnp.sum(jnp.where(own_column, back_imag, 0.0), axis=1, keepdims=True)
        scale = weight[direction]
        z_real += scale * (
            real * diag_real + imag * diag_imag - (back_real * row_real + back_imag * row_imag)
        )
        z_imag += scale * (
            imag * diag_real - real * diag_imag - (back_imag * row_real - back_real * row_imag)
        )
    zrows[p, 0:16, :] = z_real
    zrows[p, 16:32, :] = z_imag

    def z_copy(j):
        dest = (q + j) % NQ * 2 + core
        return remote(zrows.at[p], zrows.at[p], z_send.at[j], z_recv.at[j], k, dest)

    def z_share(j):
        owner = (q + NQ - j) % NQ * 2 + core
        return remote(zrows.at[owner], zrows.at[owner], zz_send.at[j], zz_recv.at[j], k, sibling)

    @pl.loop(1, NQ)
    def _(j):
        z_copy(j).start()

    z_share(0).start()

    @pl.loop(1, NQ)
    def _(j):
        owner = (q + NQ - j) % NQ * 2 + core
        remote(zrows.at[owner], zrows.at[owner], z_send.at[j], z_recv.at[j], k, sibling).wait_recv()
        z_share(j).start()

    @pl.loop(0, NQ)
    def _(j):
        owner = (q + NQ - j) % NQ * 2 + 1 - core
        remote(zrows.at[owner], zrows.at[owner], zz_send.at[j], zz_recv.at[j], k, sibling).wait_recv()

    real = zrows[:, 0:16, :].reshape(NB, NB)
    imag = zrows[:, 16:32, :].reshape(NB, NB)
    grad_out[0] = 0.5 * (real - real.T)
    grad_out[1] = 0.5 * (imag + imag.T)

    for h in range(HOPS):
        list_copy(h).wait_send()
    other_copy.wait_send()

    @pl.loop(0, CHUNKS)
    def _(c):
        own_copy(c, stream.at[0, :, blocks(c)]).wait_send()
        for h in range(1, HOPS):
            hop_copy(h, c).wait_send()

    def sent(slot):
        @pl.loop(1, NQ)
        def _(j):
            part_copy(slot, j).wait_send()

        for copy in end_copies(slot)[1]:
            copy.wait_send()

    for on in range(2):
        @pl.when(core == on)
        def _():
            for h in range(2):
                @pl.loop(1, NQ)
                def _(j):
                    a_part_copy(on, h, j).wait_send()

                for copy in a_end_copies(on, h):
                    copy.wait_send()

    sent(C)

    @pl.when(b_here)
    def _():
        sent(B)

    @pl.when(w_here)
    def _():
        sent(W)

    z_share(0).wait_send()

    @pl.loop(1, NQ)
    def _(j):
        z_copy(j).wait_send()
        z_share(j).wait_send()


def local(wave, wave_perm, shell_weight):
    dma = pltpu.SemaphoreType.DMA
    vmem = pl.BlockSpec(memory_space=pltpu.VMEM)
    correlation, gradient = pl.pallas_call(
        kernel,
        out_shape=(
            jax.ShapeDtypeStruct((3, 2, 16, NB), jnp.float32),
            jax.ShapeDtypeStruct((2, NB, NB), jnp.float32),
        ),
        in_specs=[pl.BlockSpec(memory_space=pl.ANY)] * 3 + [pl.BlockSpec(memory_space=pltpu.SMEM)],
        out_specs=(vmem, vmem),
        scratch_shapes=[
            pltpu.VMEM((2, 16, 16, NG), jnp.bfloat16),
            pltpu.VMEM((HOPS, 2, 16, 16, NG), jnp.bfloat16),
            pltpu.VMEM((2, 16, 16, NG), jnp.bfloat16),
            pltpu.VMEM((4, 2 * NB, NG), jnp.bfloat16),
            pltpu.VMEM((2, NB, NB), jnp.float32),
            pltpu.VMEM((HOPS + 1, 3, 1, NG), jnp.int32),
            pltpu.VMEM((4, NQ, BLOCK, NB), jnp.float32),
            pltpu.VMEM((4, NQ, BLOCK, NB), jnp.float32),
            pltpu.VMEM((4, 2, HALF, NB), jnp.float32),
            pltpu.VMEM((3, 2, 2, HALF, NB), jnp.float32),
            pltpu.VMEM((2 * NQ, 32, NB), jnp.float32),
            dma((HOPS, CHUNKS)), dma((HOPS, CHUNKS)), dma, dma, dma((HOPS,)), dma((HOPS,)),
            dma((5, NQ)), dma((5, NQ)), dma((5, 3)), dma((3, 2, 2)),
            dma((NQ,)), dma((NQ,)), dma((NQ,)), dma((NQ,)), dma, dma,
            pltpu.SemaphoreType.REGULAR((4,)),
        ],
        compiler_params=pltpu.CompilerParams(
            collective_id=0, has_side_effects=True, vmem_limit_bytes=48 * 1024 * 1024
        ),
        cost_estimate=pl.CostEstimate(
            flops=2 * 4 * 512 * NG * (NG + 512), bytes_accessed=4 * 512 * NG, transcendentals=0
        ),
    )(
        pltpu.with_memory_space_constraint(wave.reshape(2, 16, 16, NG), pltpu.HBM),
        pltpu.with_memory_space_constraint(wave.reshape(2, NQ, 2, 16, NG), pltpu.HBM),
        pltpu.with_memory_space_constraint(wave_perm[0][:, None, :], pltpu.HBM),
        pltpu.with_memory_space_constraint(shell_weight, pltpu.HBM),
    )
    return correlation[None], gradient[None]


def solution(mesh):
    placed = (P("ka", None, None, "pw"), P("ka", None, "pw"), P())
    return jax.shard_map(
        local,
        mesh=mesh,
        in_specs=placed,
        out_specs=(P("ka", None, None, "pw", None), P("ka", None, None, None)),
        check_vma=False,
    )
```

```python
import jax
import jax.numpy as jnp
from jax import lax
from jax.experimental import pallas as pl
from jax.experimental.pallas import tpu as pltpu
from jax.sharding import PartitionSpec as P

MESH = pl.DeviceIdType.MESH
NK = 32
NB = 256
NG = 1280
NQ = 8
HOPS = 4
CHUNKS = 4
ROWS = NB // CHUNKS
BLOCKS = ROWS // 16
A, B, W, C = range(4)
BLOCK = 72
HALF = 40


def kernel(
    wave_in, wave_halves, perm, weight_in, corr_out, grad_out,
    weight, wave, stream, other, turned, product, lists, part, gathered, reduced, ends, zrows,
    stream_send, stream_recv, other_send, other_recv, list_send, list_recv,
    part_send, part_recv, end_send, end_recv, z_send, z_recv, zz_send, zz_recv, wave_sem, list_sem, weight_sem, told,
):
    k = lax.axis_index("ka")
    p = lax.axis_index("pw")
    core = p % 2
    q = p // 2
    sibling = p + 1 - 2 * core
    level = k // 2 % 4
    group = k // 8 * 8
    inner = k % 8
    to_next = (k + 30 + 4 * core) % NK
    a_up, a_down = (k + 8) % NK, (k + 24) % NK
    b_up, b_down = group + (inner + 2) % 8, group + (inner + 6) % 8
    flip = k + 1 - 2 * (k % 2)
    a_end = (k + 8 + 16 * core) % NK
    b_end = group + (inner + 2 + 4 * core) % 8
    w_end = group + (inner + 6 - 4 * core) % 8
    b_here = level != 3 - 3 * core
    w_here = level == 3 * core

    def remote(src, dst, send_sem, recv_sem, ka, pw):
        return pltpu.make_async_remote_copy(
            src_ref=src, dst_ref=dst, send_sem=send_sem, recv_sem=recv_sem,
            device_id=(ka, pw), device_id_type=MESH,
        )

    around = [
        ((k + 2) % NK, p), ((k + 30) % NK, p), (flip, p), (flip, (q + 4) % NQ * 2 + core),
        (k, (q // 4 * 4 + (q + 1) % 4) * 2 + core), (k, (q // 4 * 4 + (q + 3) % 4) * 2 + core), (k, sibling),
    ]

    def tell(sem):
        for neighbour in around:
            pl.semaphore_signal(sem, inc=1, device_id=neighbour, device_id_type=MESH)

    barrier = pltpu.get_barrier_semaphore()
    tell(barrier)
    wave_copy = pltpu.make_async_copy(wave_in, wave, wave_sem)
    own_list_copy = pltpu.make_async_copy(perm, lists.at[0], list_sem)
    weight_copy = pltpu.make_async_copy(weight_in, weight, weight_sem)
    wave_copy.start()
    own_list_copy.start()
    weight_copy.start()
    pl.semaphore_wait(barrier, len(around))

    def blocks(c):
        return pl.ds(c * BLOCKS, BLOCKS)

    def own_copy(c, source):
        return remote(
            source, stream.at[0, :, blocks(c)],
            stream_send.at[0, c], stream_recv.at[0, c], to_next, p,
        )

    def hop_copy(h, c):
        return remote(
            stream.at[h - 1, :, blocks(c)], stream.at[h, :, blocks(c)],
            stream_send.at[h, c], stream_recv.at[h, c], to_next, p,
        )

    def list_copy(h):
        source = perm if h == 0 else lists.at[h]
        return remote(
            source.at[0:2], lists.at[h + 1, 0:2], list_send.at[h], list_recv.at[h], to_next, p
        )

    other_copy = remote(wave_in, other, other_send, other_recv, flip, p)

    list_copy(0).start()

    @pl.when(core == 0)
    def _():
        for c in range(CHUNKS):
            own_copy(c, wave_in.at[:, blocks(c)]).start()

    @pl.when(core == 1)
    def _():
        for c in range(CHUNKS):
            own_copy(c, wave_halves.at[:, c % 2 * 4:c % 2 * 4 + 4, c // 2]).start()

    other_copy.start()
    tell(told.at[0])
    own_list_copy.wait()
    wave_copy.wait()
    weight_copy.wait()

    def turn_start(slot, direction):
        @pl.loop(0, NG // 256)
        def _(j):
            row = lists[0, direction] - p * NG
            wanted = lax.broadcasted_iota(jnp.int32, (256, NG), 0) + j * 256
            pick = jnp.where(wanted == row, 1.0, 0.0).astype(jnp.bfloat16)
            value = lax.dot_general(
                wave[...].reshape(2 * NB, NG), pick, (((1,), (1,)), ((), ())),
                preferred_element_type=jnp.float32,
            )
            turned[slot, :, pl.ds(pl.multiple_of(j * 256, 256), 256)] = value.astype(jnp.bfloat16)

    def turn_end(slot, direction, hops):
        @pl.loop(0, NG // 256)
        def _(j):
            columns = pl.ds(pl.multiple_of(j * 256, 256), 256)
            row = lists[hops, direction, :, columns] - p * NG
            held = lax.broadcasted_iota(jnp.int32, (NG, 256), 0)
            pick = jnp.where(held == row, 1.0, 0.0).astype(jnp.bfloat16)
            value = lax.dot_general(
                wave[...].reshape(2 * NB, NG), pick, (((1,), (0,)), ((), ())),
                preferred_element_type=jnp.float32,
            )
            turned[slot, :, columns] = value.astype(jnp.bfloat16)

    def multiply(slot, source, c, order):
        value = lax.dot_general(
            source[:, blocks(c)].reshape(2 * ROWS, NG), turned[slot], (((1,), (1,)), ((), ())),
            preferred_element_type=jnp.float32,
        )
        real = value[:ROWS, :NB] + value[ROWS:, NB:]
        imag = value[:ROWS, NB:] - value[ROWS:, :NB]
        for i in range(BLOCKS):
            n = c * BLOCKS + i
            block = n + order * (n % NQ * 2 + n // NQ - n)
            rows = pl.ds(pl.multiple_of(block * 16, 16), 16)
            product[0, rows, :] = real[16 * i:16 * i + 16]
            product[1, rows, :] = imag[16 * i:16 * i + 16]

    def part_copy(slot, j):
        dest = (q + j) % NQ
        return remote(
            part.at[slot, dest], gathered.at[slot, j],
            part_send.at[slot, j], part_recv.at[slot, j], k, dest * 2 + core,
        )

    def hand_out(slot, at_start):
        swap = jnp.broadcast_to(at_start, (NB, NB)) > 0
        real, imag = product[0], product[1]
        real = jnp.where(swap, real.T, real)
        imag = jnp.where(swap, -imag.T, imag)
        eye = lax.broadcasted_iota(jnp.int32, (NB, NB), 0) == lax.broadcasted_iota(jnp.int32, (NB, NB), 1)
        diag_real = jnp.sum(jnp.where(eye, real, 0.0), axis=0, keepdims=True)
        diag_imag = jnp.sum(jnp.where(eye, imag, 0.0), axis=0, keepdims=True)
        first = lax.broadcasted_iota(jnp.int32, (8, NB), 0) < 4
        diag = jnp.where(first, diag_real, diag_imag)
        real = real.reshape(NQ, 2, 16, NB)
        imag = imag.reshape(NQ, 2, 16, NB)
        part[slot, :, 0:16, :] = real[:, 0]
        part[slot, :, 16:32, :] = imag[:, 0]
        part[slot, :, 32:48, :] = real[:, 1]
        part[slot, :, 48:64, :] = imag[:, 1]
        part[slot, :, 64:72, :] = jnp.broadcast_to(diag[None], (NQ, 8, NB))

        @pl.loop(1, NQ)
        def _(j):
            part_copy(slot, j).start()

    def end_copies(slot):
        if slot == C:
            direction, role, far_role, end, near, far = 2, 0, 1, flip, core, core
        elif slot == W:
            direction, role, far_role, end, near, far = 1, 1 - core, core, w_end, 0, 1
        else:
            direction, role, far_role, end, near, far = 1, core, 1 - core, b_end, 0, 1
        local = (direction, role, near)
        target = ends.at[direction, far_role, far]
        sem = end_recv.at[direction, far_role, far]
        copies = [
            remote(
                reduced.at[slot, 1 - core], ends.at[direction, role, near],
                end_send.at[slot, 0], end_recv.at[direction, role, near], k, sibling,
            ),
            remote(reduced.at[slot, 0], target, end_send.at[slot, 1], sem, end, 2 * q),
            remote(reduced.at[slot, 1], target, end_send.at[slot, 2], sem, end, 2 * q + 1),
        ]
        return local, copies

    def pass_on(slot):
        @pl.loop(1, NQ)
        def _(j):
            part_copy(slot, j).wait_recv()

        total = part[slot, q]
        for j in range(1, NQ):
            total = total + gathered[slot, j]
        reduced[slot, 0, 0:32, :] = total[0:32]
        reduced[slot, 0, 32:40, :] = total[64:72]
        reduced[slot, 1, 0:32, :] = total[32:64]
        reduced[slot, 1, 32:40, :] = total[64:72]
        local, copies = end_copies(slot)
        for copy in copies:
            copy.start()
        ends[local[0], local[1], local[2]] = reduced[slot, core]

    def a_piece(ref, on, h):
        if on == 0:
            return ref.at[:, 128 * h:128 * h + 128]
        return ref.at[32 * h:(32, BLOCK)[h], :]

    def a_part_copy(on, h, j):
        dest = (q + j) % NQ
        row = (4, A)[h]
        return remote(
            a_piece(part.at[A, dest], on, h), a_piece(gathered.at[A, j], on, h),
            part_send.at[row, j], part_recv.at[row, j], k, dest * 2 + core,
        )

    def a_diag(real, imag, h):
        shape = real.shape
        eye = (
            lax.broadcasted_iota(jnp.int32, shape, 0) == lax.broadcasted_iota(jnp.int32, shape, 1) + 128 * h
        )
        diag_real = jnp.sum(jnp.where(eye, real, 0.0), axis=0, keepdims=True)
        diag_imag = jnp.sum(jnp.where(eye, imag, 0.0), axis=0, keepdims=True)
        first = lax.broadcasted_iota(jnp.int32, (8, shape[1]), 0) < 4
        return jnp.broadcast_to(jnp.where(first, diag_real, diag_imag)[None], (NQ, 8, shape[1]))

    def a_hand_out(h):
        @pl.when(core == 0)
        def _():
            columns = slice(128 * h, 128 * h + 128)
            real = product[0, columns, :].T
            imag = -product[1, columns, :].T
            part[A, :, 64:72, columns] = a_diag(real, imag, h)
            real = real.reshape(NQ, 2, 16, 128)
            imag = imag.reshape(NQ, 2, 16, 128)
            for i in range(2):
                part[A, :, 32 * i:32 * i + 16, columns] = real[:, i]
                part[A, :, 32 * i + 16:32 * i + 32, columns] = imag[:, i]

            @pl.loop(1, NQ)
            def _(j):
                a_part_copy(0, h, j).start()

        @pl.when(core == 1)
        def _():
            real, imag = product[0], product[1]
            if h == 1:
                part[A, :, 64:72, :] = a_diag(real, imag, 0)
            part[A, :, 32 * h:32 * h + 16, :] = real.reshape(NQ, 2, 16, NB)[:, h]
            part[A, :, 32 * h + 16:32 * h + 32, :] = imag.reshape(NQ, 2, 16, NB)[:, h]

            @pl.loop(1, NQ)
            def _(j):
                a_part_copy(1, h, j).start()

    def a_end_copies(on, h):
        near, near_sem = ends.at[0, on, 0], end_recv.at[0, on, 0]
        far, far_sem = ends.at[0, 1 - on, 1], end_recv.at[0, 1 - on, 1]
        row = (4, A)[h]
        if on == 0:
            rows, columns = slice(0, HALF), slice(128 * h, 128 * h + 128)
            last = [(1, near, near_sem, k, sibling), (1, far, far_sem, a_end, 2 * q + 1)]
            todo = last + [(0, far, far_sem, a_end, 2 * q)]
            cuts = [(rows, columns)] * 3
        else:
            rows, columns = slice(32 * h, (32, HALF)[h]), slice(0, NB)
            todo = [(0, near, near_sem, k, sibling), (0, far, far_sem, a_end, 2 * q)]
            cuts = [(rows, columns)] * 2
            if h == 1:
                todo = todo + [(1, far, far_sem, a_end, 2 * q + 1)]
                cuts = cuts + [(slice(0, HALF), columns)]
        return [
            remote(
                reduced.at[A, half, cut[0], cut[1]], target.at[cut[0], cut[1]],
                end_send.at[row, i], sem, ka, pw,
            )
            for i, ((half, target, sem, ka, pw), cut) in enumerate(zip(todo, cuts))
        ]

    def a_pass_on(h):
        for on in range(2):
            @pl.when(core == on)
            def _():
                @pl.loop(1, NQ)
                def _(j):
                    a_part_copy(on, h, j).wait_recv()

                total = a_piece(part.at[A, q], on, h)[...]
                for j in range(1, NQ):
                    total = total + a_piece(gathered.at[A, j], on, h)[...]
                if on == 0:
                    columns = slice(128 * h, 128 * h + 128)
                    for half in range(2):
                        reduced[A, half, 0:32, columns] = total[32 * half:32 * half + 32]
                        reduced[A, half, 32:40, columns] = total[64:72]
                else:
                    reduced[A, h, 0:32, :] = total[0:32]
                    if h == 1:
                        reduced[A, 0, 32:40, :] = total[32:40]
                        reduced[A, 1, 32:40, :] = total[32:40]
                for copy in a_end_copies(on, h):
                    copy.start()

        if h == 1:
            ends[0, core, 0] = reduced[A, core]

    turn_start(C, 2)
    list_copy(0).wait_recv()
    list_copy(1).start()
    for c in range(CHUNKS):
        own_copy(c, stream.at[0, :, blocks(c)]).wait_recv()
        hop_copy(1, c).start()
        pl.semaphore_wait(told.at[c], len(around))
        if c < CHUNKS - 1:
            tell(told.at[c + 1])

    @pl.when(b_here)
    def _():
        @pl.when(core == 0)
        def _():
            turn_start(B, 1)

        @pl.when(core == 1)
        def _():
            turn_end(B, 1, 1)

        @pl.loop(0, CHUNKS)
        def _(c):
            multiply(B, stream.at[0], c, core)

        hand_out(B, 1 - core)

    list_copy(1).wait_recv()
    list_copy(2).start()

    @pl.when(core == 0)
    def _():
        turn_start(A, 0)

    @pl.loop(0, CHUNKS)
    def _(c):
        hop_copy(1, c).wait_recv()
        hop_copy(2, c).start()

    other_copy.wait_recv()

    @pl.loop(0, CHUNKS)
    def _(c):
        multiply(C, other, c, 0)

    hand_out(C, 1)

    list_copy(2).wait_recv()
    list_copy(3).start()

    @pl.when(w_here)
    def _():
        @pl.when(core == 0)
        def _():
            turn_end(W, 1, 3)

        @pl.when(core == 1)
        def _():
            turn_start(W, 1)
    @pl.loop(0, CHUNKS)
    def _(c):
        hop_copy(2, c).wait_recv()
        hop_copy(3, c).start()

    @pl.when(w_here)
    def _():
        @pl.loop(0, CHUNKS)
        def _(c):
            multiply(W, stream.at[2], c, core)

        hand_out(W, core)

    pass_on(C)

    list_copy(3).wait_recv()

    @pl.when(core == 1)
    def _():
        turn_end(A, 0, 4)

    @pl.loop(0, CHUNKS // 2)
    def _(c):
        hop_copy(3, c).wait_recv()
        multiply(A, stream.at[3], c, core)

    a_hand_out(0)

    @pl.loop(CHUNKS // 2, CHUNKS)
    def _(c):
        hop_copy(3, c).wait_recv()
        multiply(A, stream.at[3], c, core)

    a_hand_out(1)

    @pl.when(b_here)
    def _():
        pass_on(B)

    @pl.when(w_here)
    def _():
        pass_on(W)

    a_pass_on(0)
    a_pass_on(1)

    def arrived(direction, role, place):
        ref = ends.at[direction, role, place]
        remote(ref, ref, end_send.at[A, 0], end_recv.at[direction, role, place], k, sibling).wait_recv()

    arrived(2, 0, 1 - core)
    arrived(2, 1, 0)
    arrived(2, 1, 1)
    arrived(1, 0, 1)
    arrived(1, 1, 1)

    @pl.when(core != level // 3)
    def _():
        arrived(1, 0, 0)

    @pl.when(core != (level + 2) // 3)
    def _():
        arrived(1, 1, 0)

    arrived(0, 1 - core, 0)
    arrived(0, 0, 1)
    arrived(0, 1, 1)

    z_real = jnp.zeros((16, NB), jnp.float32)
    z_imag = jnp.zeros((16, NB), jnp.float32)
    own_column = (
        lax.broadcasted_iota(jnp.int32, (16, NB), 0) + p * 16 == lax.broadcasted_iota(jnp.int32, (16, NB), 1)
    )
    for direction in range(3):
        ahead = ends[direction, 0, 0] + ends[direction, 0, 1]
        behind = ends[direction, 1, 0] + ends[direction, 1, 1]
        real, imag = ahead[0:16], ahead[16:32]
        diag_real, diag_imag = ahead[32:33], ahead[36:37]
        corr_out[direction, 0] = real
        corr_out[direction, 1] = imag
        back_real, back_imag = behind[0:16], behind[16:32]
        row_real = jnp.sum(jnp.where(own_column, back_real, 0.0), axis=1, keepdims=True)
        row_imag = jnp.sum(jnp.where(own_column, back_imag, 0.0), axis=1, keepdims=True)
        scale = weight[direction]
        z_real += scale * (
            real * diag_real + imag * diag_imag - (back_real * row_real + back_imag * row_imag)
        )
        z_imag += scale * (
            imag * diag_real - real * diag_imag - (back_imag * row_real - back_real * row_imag)
        )
    zrows[p, 0:16, :] = z_real
    zrows[p, 16:32, :] = z_imag

    def z_copy(j):
        dest = (q + j) % NQ * 2 + core
        return remote(zrows.at[p], zrows.at[p], z_send.at[j], z_recv.at[j], k, dest)

    def z_share(j):
        owner = (q + NQ - j) % NQ * 2 + core
        return remote(zrows.at[owner], zrows.at[owner], zz_send.at[j], zz_recv.at[j], k, sibling)

    @pl.loop(1, NQ)
    def _(j):
        z_copy(j).start()

    z_share(0).start()

    @pl.loop(1, NQ)
    def _(j):
        owner = (q + NQ - j) % NQ * 2 + core
        remote(zrows.at[owner], zrows.at[owner], z_send.at[j], z_recv.at[j], k, sibling).wait_recv()
        z_share(j).start()

    @pl.loop(0, NQ)
    def _(j):
        owner = (q + NQ - j) % NQ * 2 + 1 - core
        remote(zrows.at[owner], zrows.at[owner], zz_send.at[j], zz_recv.at[j], k, sibling).wait_recv()

    real = zrows[:, 0:16, :].reshape(NB, NB)
    imag = zrows[:, 16:32, :].reshape(NB, NB)
    grad_out[0] = 0.5 * (real - real.T)
    grad_out[1] = 0.5 * (imag + imag.T)

    for h in range(HOPS):
        list_copy(h).wait_send()
    other_copy.wait_send()

    @pl.loop(0, CHUNKS)
    def _(c):
        own_copy(c, stream.at[0, :, blocks(c)]).wait_send()
        for h in range(1, HOPS):
            hop_copy(h, c).wait_send()

    def sent(slot):
        @pl.loop(1, NQ)
        def _(j):
            part_copy(slot, j).wait_send()

        for copy in end_copies(slot)[1]:
            copy.wait_send()

    for on in range(2):
        @pl.when(core == on)
        def _():
            for h in range(2):
                @pl.loop(1, NQ)
                def _(j):
                    a_part_copy(on, h, j).wait_send()

                for copy in a_end_copies(on, h):
                    copy.wait_send()

    sent(C)

    @pl.when(b_here)
    def _():
        sent(B)

    @pl.when(w_here)
    def _():
        sent(W)

    z_share(0).wait_send()

    @pl.loop(1, NQ)
    def _(j):
        z_copy(j).wait_send()
        z_share(j).wait_send()


def local(wave, wave_perm, shell_weight):
    dma = pltpu.SemaphoreType.DMA
    vmem = pl.BlockSpec(memory_space=pltpu.VMEM)
    correlation, gradient = pl.pallas_call(
        kernel,
        out_shape=(
            jax.ShapeDtypeStruct((3, 2, 16, NB), jnp.float32),
            jax.ShapeDtypeStruct((2, NB, NB), jnp.float32),
        ),
        in_specs=[pl.BlockSpec(memory_space=pl.ANY)] * 4,
        out_specs=(vmem, vmem),
        scratch_shapes=[
            pltpu.SMEM((3,), jnp.float32),
            pltpu.VMEM((2, 16, 16, NG), jnp.bfloat16),
            pltpu.VMEM((HOPS, 2, 16, 16, NG), jnp.bfloat16),
            pltpu.VMEM((2, 16, 16, NG), jnp.bfloat16),
            pltpu.VMEM((4, 2 * NB, NG), jnp.bfloat16),
            pltpu.VMEM((2, NB, NB), jnp.float32),
            pltpu.VMEM((HOPS + 1, 3, 1, NG), jnp.int32),
            pltpu.VMEM((4, NQ, BLOCK, NB), jnp.float32),
            pltpu.VMEM((4, NQ, BLOCK, NB), jnp.float32),
            pltpu.VMEM((4, 2, HALF, NB), jnp.float32),
            pltpu.VMEM((3, 2, 2, HALF, NB), jnp.float32),
            pltpu.VMEM((2 * NQ, 32, NB), jnp.float32),
            dma((HOPS, CHUNKS)), dma((HOPS, CHUNKS)), dma, dma, dma((HOPS,)), dma((HOPS,)),
            dma((5, NQ)), dma((5, NQ)), dma((5, 3)), dma((3, 2, 2)),
            dma((NQ,)), dma((NQ,)), dma((NQ,)), dma((NQ,)), dma, dma,
            dma, pltpu.SemaphoreType.REGULAR((4,)),
        ],
        compiler_params=pltpu.CompilerParams(
            collective_id=0, has_side_effects=True, vmem_limit_bytes=48 * 1024 * 1024
        ),
        cost_estimate=pl.CostEstimate(
            flops=2 * 4 * 512 * NG * (NG + 512), bytes_accessed=4 * 512 * NG, transcendentals=0
        ),
    )(
        pltpu.with_memory_space_constraint(wave.reshape(2, 16, 16, NG), pltpu.HBM),
        pltpu.with_memory_space_constraint(wave.reshape(2, NQ, 2, 16, NG), pltpu.HBM),
        pltpu.with_memory_space_constraint(wave_perm[0][:, None, :], pltpu.HBM),
        pltpu.with_memory_space_constraint(shell_weight, pltpu.HBM),
    )
    return correlation[None], gradient[None]


def solution(mesh):
    placed = (P("ka", None, None, "pw"), P("ka", None, "pw"), P())
    return jax.shard_map(
        local,
        mesh=mesh,
        in_specs=placed,
        out_specs=(P("ka", None, None, "pw", None), P("ka", None, None, None)),
        check_vma=False,
    )
```

```python
import jax
import jax.numpy as jnp
from jax import lax
from jax.experimental import pallas as pl
from jax.experimental.pallas import tpu as pltpu
from jax.sharding import PartitionSpec as P

MESH = pl.DeviceIdType.MESH
NK = 32
NB = 256
NG = 1280
NQ = 8
HOPS = 4
FAR_FIRST = (6, 5, 7, 2, 4, 1, 3)
CHUNKS = 4
ROWS = NB // CHUNKS
BLOCKS = ROWS // 16
A, B, W, C = range(4)
BLOCK = 72
HALF = 40


def kernel(
    wave_in, wave_halves, perm, weight_in, corr_out, grad_out,
    weight, wave, stream, other, turned, product, lists, part, gathered, reduced, ends, zrows,
    stream_send, stream_recv, other_send, other_recv, list_send, list_recv,
    part_send, part_recv, end_send, end_recv, z_send, z_recv, zz_send, zz_recv, wave_sem, list_sem, weight_sem, told,
):
    k = lax.axis_index("ka")
    p = lax.axis_index("pw")
    core = p % 2
    q = p // 2
    sibling = p + 1 - 2 * core
    level = k // 2 % 4
    group = k // 8 * 8
    inner = k % 8
    to_next = (k + 30 + 4 * core) % NK
    a_up, a_down = (k + 8) % NK, (k + 24) % NK
    b_up, b_down = group + (inner + 2) % 8, group + (inner + 6) % 8
    flip = k + 1 - 2 * (k % 2)
    a_end = (k + 8 + 16 * core) % NK
    b_end = group + (inner + 2 + 4 * core) % 8
    w_end = group + (inner + 6 - 4 * core) % 8
    b_here = level != 3 - 3 * core
    w_here = level == 3 * core

    def remote(src, dst, send_sem, recv_sem, ka, pw):
        return pltpu.make_async_remote_copy(
            src_ref=src, dst_ref=dst, send_sem=send_sem, recv_sem=recv_sem,
            device_id=(ka, pw), device_id_type=MESH,
        )

    around = [
        ((k + 2) % NK, p), ((k + 30) % NK, p), (flip, p), (flip, (q + 4) % NQ * 2 + core),
        (k, (q // 4 * 4 + (q + 1) % 4) * 2 + core), (k, (q // 4 * 4 + (q + 3) % 4) * 2 + core), (k, sibling),
    ]

    def tell(sem):
        for neighbour in around:
            pl.semaphore_signal(sem, inc=1, device_id=neighbour, device_id_type=MESH)

    barrier = pltpu.get_barrier_semaphore()
    tell(barrier)
    wave_copy = pltpu.make_async_copy(wave_in, wave, wave_sem)
    own_list_copy = pltpu.make_async_copy(perm, lists.at[0], list_sem)
    weight_copy = pltpu.make_async_copy(weight_in, weight, weight_sem)
    wave_copy.start()
    own_list_copy.start()
    weight_copy.start()
    pl.semaphore_wait(barrier, len(around))

    def blocks(c):
        return pl.ds(c * BLOCKS, BLOCKS)

    def own_copy(c, source):
        return remote(
            source, stream.at[0, :, blocks(c)],
            stream_send.at[0, c], stream_recv.at[0, c], to_next, p,
        )

    def hop_copy(h, c):
        return remote(
            stream.at[h - 1, :, blocks(c)], stream.at[h, :, blocks(c)],
            stream_send.at[h, c], stream_recv.at[h, c], to_next, p,
        )

    def list_copy(h):
        source = perm if h == 0 else lists.at[h]
        return remote(
            source.at[0:2], lists.at[h + 1, 0:2], list_send.at[h], list_recv.at[h], to_next, p
        )

    other_copy = remote(wave_in, other, other_send, other_recv, flip, p)

    list_copy(0).start()

    @pl.when(core == 0)
    def _():
        for c in range(CHUNKS):
            own_copy(c, wave_in.at[:, blocks(c)]).start()

    @pl.when(core == 1)
    def _():
        for c in range(CHUNKS):
            own_copy(c, wave_halves.at[:, c % 2 * 4:c % 2 * 4 + 4, c // 2]).start()

    other_copy.start()
    tell(told.at[0])
    own_list_copy.wait()
    wave_copy.wait()
    weight_copy.wait()

    def turn_start(slot, direction):
        @pl.loop(0, NG // 256)
        def _(j):
            row = lists[0, direction] - p * NG
            wanted = lax.broadcasted_iota(jnp.int32, (256, NG), 0) + j * 256
            pick = jnp.where(wanted == row, 1.0, 0.0).astype(jnp.bfloat16)
            value = lax.dot_general(
                wave[...].reshape(2 * NB, NG), pick, (((1,), (1,)), ((), ())),
                preferred_element_type=jnp.float32,
            )
            turned[slot, :, pl.ds(pl.multiple_of(j * 256, 256), 256)] = value.astype(jnp.bfloat16)

    def turn_end(slot, direction, hops):
        @pl.loop(0, NG // 256)
        def _(j):
            columns = pl.ds(pl.multiple_of(j * 256, 256), 256)
            row = lists[hops, direction, :, columns] - p * NG
            held = lax.broadcasted_iota(jnp.int32, (NG, 256), 0)
            pick = jnp.where(held == row, 1.0, 0.0).astype(jnp.bfloat16)
            value = lax.dot_general(
                wave[...].reshape(2 * NB, NG), pick, (((1,), (0,)), ((), ())),
                preferred_element_type=jnp.float32,
            )
            turned[slot, :, columns] = value.astype(jnp.bfloat16)

    def multiply(slot, source, c, order):
        value = lax.dot_general(
            source[:, blocks(c)].reshape(2 * ROWS, NG), turned[slot], (((1,), (1,)), ((), ())),
            preferred_element_type=jnp.float32,
        )
        real = value[:ROWS, :NB] + value[ROWS:, NB:]
        imag = value[:ROWS, NB:] - value[ROWS:, :NB]
        for i in range(BLOCKS):
            n = c * BLOCKS + i
            block = n + order * (n % NQ * 2 + n // NQ - n)
            rows = pl.ds(pl.multiple_of(block * 16, 16), 16)
            product[0, rows, :] = real[16 * i:16 * i + 16]
            product[1, rows, :] = imag[16 * i:16 * i + 16]

    def part_copy(slot, j):
        dest = (q + j) % NQ
        return remote(
            part.at[slot, dest], gathered.at[slot, j],
            part_send.at[slot, j], part_recv.at[slot, j], k, dest * 2 + core,
        )

    def hand_out(slot, at_start):
        swap = jnp.broadcast_to(at_start, (NB, NB)) > 0
        real, imag = product[0], product[1]
        real = jnp.where(swap, real.T, real)
        imag = jnp.where(swap, -imag.T, imag)
        eye = lax.broadcasted_iota(jnp.int32, (NB, NB), 0) == lax.broadcasted_iota(jnp.int32, (NB, NB), 1)
        diag_real = jnp.sum(jnp.where(eye, real, 0.0), axis=0, keepdims=True)
        diag_imag = jnp.sum(jnp.where(eye, imag, 0.0), axis=0, keepdims=True)
        first = lax.broadcasted_iota(jnp.int32, (8, NB), 0) < 4
        diag = jnp.where(first, diag_real, diag_imag)
        real = real.reshape(NQ, 2, 16, NB)
        imag = imag.reshape(NQ, 2, 16, NB)
        part[slot, :, 0:16, :] = real[:, 0]
        part[slot, :, 16:32, :] = imag[:, 0]
        part[slot, :, 32:48, :] = real[:, 1]
        part[slot, :, 48:64, :] = imag[:, 1]
        part[slot, :, 64:72, :] = jnp.broadcast_to(diag[None], (NQ, 8, NB))

        @pl.loop(1, NQ)
        def _(j):
            part_copy(slot, j).start()

    def end_copies(slot):
        if slot == C:
            direction, role, far_role, end, near, far = 2, 0, 1, flip, core, core
        elif slot == W:
            direction, role, far_role, end, near, far = 1, 1 - core, core, w_end, 0, 1
        else:
            direction, role, far_role, end, near, far = 1, core, 1 - core, b_end, 0, 1
        local = (direction, role, near)
        target = ends.at[direction, far_role, far]
        sem = end_recv.at[direction, far_role, far]
        copies = [
            remote(
                reduced.at[slot, 1 - core], ends.at[direction, role, near],
                end_send.at[slot, 0], end_recv.at[direction, role, near], k, sibling,
            ),
            remote(reduced.at[slot, 0], target, end_send.at[slot, 1], sem, end, 2 * q),
            remote(reduced.at[slot, 1], target, end_send.at[slot, 2], sem, end, 2 * q + 1),
        ]
        return local, copies

    def pass_on(slot):
        @pl.loop(1, NQ)
        def _(j):
            part_copy(slot, j).wait_recv()

        total = part[slot, q]
        for j in range(1, NQ):
            total = total + gathered[slot, j]
        reduced[slot, 0, 0:32, :] = total[0:32]
        reduced[slot, 0, 32:40, :] = total[64:72]
        reduced[slot, 1, 0:32, :] = total[32:64]
        reduced[slot, 1, 32:40, :] = total[64:72]
        local, copies = end_copies(slot)
        for copy in copies:
            copy.start()
        ends[local[0], local[1], local[2]] = reduced[slot, core]

    def a_piece(ref, on, h):
        if on == 0:
            return ref.at[:, 128 * h:128 * h + 128]
        return ref.at[32 * h:(32, BLOCK)[h], :]

    def a_part_copy(on, h, j):
        dest = (q + j) % NQ
        row = (4, A)[h]
        return remote(
            a_piece(part.at[A, dest], on, h), a_piece(gathered.at[A, j], on, h),
            part_send.at[row, j], part_recv.at[row, j], k, dest * 2 + core,
        )

    def a_diag(real, imag, h):
        shape = real.shape
        eye = (
            lax.broadcasted_iota(jnp.int32, shape, 0) == lax.broadcasted_iota(jnp.int32, shape, 1) + 128 * h
        )
        diag_real = jnp.sum(jnp.where(eye, real, 0.0), axis=0, keepdims=True)
        diag_imag = jnp.sum(jnp.where(eye, imag, 0.0), axis=0, keepdims=True)
        first = lax.broadcasted_iota(jnp.int32, (8, shape[1]), 0) < 4
        return jnp.broadcast_to(jnp.where(first, diag_real, diag_imag)[None], (NQ, 8, shape[1]))

    def a_hand_out(h):
        @pl.when(core == 0)
        def _():
            columns = slice(128 * h, 128 * h + 128)
            real = product[0, columns, :].T
            imag = -product[1, columns, :].T
            part[A, :, 64:72, columns] = a_diag(real, imag, h)
            real = real.reshape(NQ, 2, 16, 128)
            imag = imag.reshape(NQ, 2, 16, 128)
            for i in range(2):
                part[A, :, 32 * i:32 * i + 16, columns] = real[:, i]
                part[A, :, 32 * i + 16:32 * i + 32, columns] = imag[:, i]

            for j in FAR_FIRST:
                a_part_copy(0, h, j).start()

        @pl.when(core == 1)
        def _():
            real, imag = product[0], product[1]
            if h == 1:
                part[A, :, 64:72, :] = a_diag(real, imag, 0)
            part[A, :, 32 * h:32 * h + 16, :] = real.reshape(NQ, 2, 16, NB)[:, h]
            part[A, :, 32 * h + 16:32 * h + 32, :] = imag.reshape(NQ, 2, 16, NB)[:, h]

            for j in FAR_FIRST:
                a_part_copy(1, h, j).start()

    def a_end_copies(on, h):
        near, near_sem = ends.at[0, on, 0], end_recv.at[0, on, 0]
        far, far_sem = ends.at[0, 1 - on, 1], end_recv.at[0, 1 - on, 1]
        row = (4, A)[h]
        if on == 0:
            rows, columns = slice(0, HALF), slice(128 * h, 128 * h + 128)
            last = [(1, near, near_sem, k, sibling), (1, far, far_sem, a_end, 2 * q + 1)]
            todo = last + [(0, far, far_sem, a_end, 2 * q)]
            cuts = [(rows, columns)] * 3
        else:
            rows, columns = slice(32 * h, (32, HALF)[h]), slice(0, NB)
            todo = [(0, near, near_sem, k, sibling), (0, far, far_sem, a_end, 2 * q)]
            cuts = [(rows, columns)] * 2
            if h == 1:
                todo = todo + [(1, far, far_sem, a_end, 2 * q + 1)]
                cuts = cuts + [(slice(0, HALF), columns)]
        return [
            remote(
                reduced.at[A, half, cut[0], cut[1]], target.at[cut[0], cut[1]],
                end_send.at[row, i], sem, ka, pw,
            )
            for i, ((half, target, sem, ka, pw), cut) in enumerate(zip(todo, cuts))
        ]

    def a_pass_on(h):
        for on in range(2):
            @pl.when(core == on)
            def _():
                @pl.loop(1, NQ)
                def _(j):
                    a_part_copy(on, h, j).wait_recv()

                total = a_piece(part.at[A, q], on, h)[...]
                for j in range(1, NQ):
                    total = total + a_piece(gathered.at[A, j], on, h)[...]
                if on == 0:
                    columns = slice(128 * h, 128 * h + 128)
                    for half in range(2):
                        reduced[A, half, 0:32, columns] = total[32 * half:32 * half + 32]
                        reduced[A, half, 32:40, columns] = total[64:72]
                else:
                    reduced[A, h, 0:32, :] = total[0:32]
                    if h == 1:
                        reduced[A, 0, 32:40, :] = total[32:40]
                        reduced[A, 1, 32:40, :] = total[32:40]
                for copy in a_end_copies(on, h):
                    copy.start()

        if h == 1:
            ends[0, core, 0] = reduced[A, core]

    turn_start(C, 2)
    list_copy(0).wait_recv()
    list_copy(1).start()
    for c in range(CHUNKS):
        own_copy(c, stream.at[0, :, blocks(c)]).wait_recv()
        hop_copy(1, c).start()
        pl.semaphore_wait(told.at[c], len(around))
        if c < CHUNKS - 1:
            tell(told.at[c + 1])

    @pl.when(b_here)
    def _():
        @pl.when(core == 0)
        def _():
            turn_start(B, 1)

        @pl.when(core == 1)
        def _():
            turn_end(B, 1, 1)

        @pl.loop(0, CHUNKS)
        def _(c):
            multiply(B, stream.at[0], c, core)

        hand_out(B, 1 - core)

    list_copy(1).wait_recv()
    list_copy(2).start()

    @pl.when(core == 0)
    def _():
        turn_start(A, 0)

    @pl.loop(0, CHUNKS)
    def _(c):
        hop_copy(1, c).wait_recv()
        hop_copy(2, c).start()

    other_copy.wait_recv()

    @pl.loop(0, CHUNKS)
    def _(c):
        multiply(C, other, c, 0)

    hand_out(C, 1)

    list_copy(2).wait_recv()
    list_copy(3).start()

    @pl.when(w_here)
    def _():
        @pl.when(core == 0)
        def _():
            turn_end(W, 1, 3)

        @pl.when(core == 1)
        def _():
            turn_start(W, 1)
    @pl.loop(0, CHUNKS)
    def _(c):
        hop_copy(2, c).wait_recv()
        hop_copy(3, c).start()

    @pl.when(w_here)
    def _():
        @pl.loop(0, CHUNKS)
        def _(c):
            multiply(W, stream.at[2], c, core)

        hand_out(W, core)

    pass_on(C)

    list_copy(3).wait_recv()

    @pl.when(core == 1)
    def _():
        turn_end(A, 0, 4)

    @pl.loop(0, CHUNKS // 2)
    def _(c):
        hop_copy(3, c).wait_recv()
        multiply(A, stream.at[3], c, core)

    a_hand_out(0)

    @pl.loop(CHUNKS // 2, CHUNKS)
    def _(c):
        hop_copy(3, c).wait_recv()
        multiply(A, stream.at[3], c, core)

    a_hand_out(1)

    @pl.when(b_here)
    def _():
        pass_on(B)

    @pl.when(w_here)
    def _():
        pass_on(W)

    a_pass_on(0)
    a_pass_on(1)

    def arrived(direction, role, place):
        ref = ends.at[direction, role, place]
        remote(ref, ref, end_send.at[A, 0], end_recv.at[direction, role, place], k, sibling).wait_recv()

    arrived(2, 0, 1 - core)
    arrived(2, 1, 0)
    arrived(2, 1, 1)
    arrived(1, 0, 1)
    arrived(1, 1, 1)

    @pl.when(core != level // 3)
    def _():
        arrived(1, 0, 0)

    @pl.when(core != (level + 2) // 3)
    def _():
        arrived(1, 1, 0)

    arrived(0, 1 - core, 0)
    arrived(0, 0, 1)
    arrived(0, 1, 1)

    z_real = jnp.zeros((16, NB), jnp.float32)
    z_imag = jnp.zeros((16, NB), jnp.float32)
    own_column = (
        lax.broadcasted_iota(jnp.int32, (16, NB), 0) + p * 16 == lax.broadcasted_iota(jnp.int32, (16, NB), 1)
    )
    for direction in range(3):
        ahead = ends[direction, 0, 0] + ends[direction, 0, 1]
        behind = ends[direction, 1, 0] + ends[direction, 1, 1]
        real, imag = ahead[0:16], ahead[16:32]
        diag_real, diag_imag = ahead[32:33], ahead[36:37]
        corr_out[direction, 0] = real
        corr_out[direction, 1] = imag
        back_real, back_imag = behind[0:16], behind[16:32]
        row_real = jnp.sum(jnp.where(own_column, back_real, 0.0), axis=1, keepdims=True)
        row_imag = jnp.sum(jnp.where(own_column, back_imag, 0.0), axis=1, keepdims=True)
        scale = weight[direction]
        z_real += scale * (
            real * diag_real + imag * diag_imag - (back_real * row_real + back_imag * row_imag)
        )
        z_imag += scale * (
            imag * diag_real - real * diag_imag - (back_imag * row_real - back_real * row_imag)
        )
    zrows[p, 0:16, :] = z_real
    zrows[p, 16:32, :] = z_imag

    def z_copy(j):
        dest = (q + j) % NQ * 2 + core
        return remote(zrows.at[p], zrows.at[p], z_send.at[j], z_recv.at[j], k, dest)

    def z_share(j):
        owner = (q + NQ - j) % NQ * 2 + core
        return remote(zrows.at[owner], zrows.at[owner], zz_send.at[j], zz_recv.at[j], k, sibling)

    for j in FAR_FIRST:
        z_copy(j).start()

    z_share(0).start()

    for h in range(HOPS):
        list_copy(h).wait_send()
    other_copy.wait_send()

    @pl.loop(0, CHUNKS)
    def _(c):
        own_copy(c, stream.at[0, :, blocks(c)]).wait_send()
        for h in range(1, HOPS):
            hop_copy(h, c).wait_send()

    def sent(slot):
        @pl.loop(1, NQ)
        def _(j):
            part_copy(slot, j).wait_send()

        for copy in end_copies(slot)[1]:
            copy.wait_send()

    for on in range(2):
        @pl.when(core == on)
        def _():
            for h in range(2):
                @pl.loop(1, NQ)
                def _(j):
                    a_part_copy(on, h, j).wait_send()

                for copy in a_end_copies(on, h):
                    copy.wait_send()

    sent(C)

    @pl.when(b_here)
    def _():
        sent(B)

    @pl.when(w_here)
    def _():
        sent(W)

    @pl.loop(1, NQ)
    def _(j):
        owner = (q + NQ - j) % NQ * 2 + core
        remote(zrows.at[owner], zrows.at[owner], z_send.at[j], z_recv.at[j], k, sibling).wait_recv()
        z_share(j).start()

    @pl.loop(0, NQ)
    def _(j):
        owner = (q + NQ - j) % NQ * 2 + 1 - core
        remote(zrows.at[owner], zrows.at[owner], zz_send.at[j], zz_recv.at[j], k, sibling).wait_recv()

    real = zrows[:, 0:16, :].reshape(NB, NB)
    imag = zrows[:, 16:32, :].reshape(NB, NB)
    grad_out[0] = 0.5 * (real - real.T)
    grad_out[1] = 0.5 * (imag + imag.T)

    z_share(0).wait_send()

    @pl.loop(1, NQ)
    def _(j):
        z_copy(j).wait_send()
        z_share(j).wait_send()


def local(wave, wave_perm, shell_weight):
    dma = pltpu.SemaphoreType.DMA
    vmem = pl.BlockSpec(memory_space=pltpu.VMEM)
    correlation, gradient = pl.pallas_call(
        kernel,
        out_shape=(
            jax.ShapeDtypeStruct((3, 2, 16, NB), jnp.float32),
            jax.ShapeDtypeStruct((2, NB, NB), jnp.float32),
        ),
        in_specs=[pl.BlockSpec(memory_space=pl.ANY)] * 4,
        out_specs=(vmem, vmem),
        scratch_shapes=[
            pltpu.SMEM((3,), jnp.float32),
            pltpu.VMEM((2, 16, 16, NG), jnp.bfloat16),
            pltpu.VMEM((HOPS, 2, 16, 16, NG), jnp.bfloat16),
            pltpu.VMEM((2, 16, 16, NG), jnp.bfloat16),
            pltpu.VMEM((4, 2 * NB, NG), jnp.bfloat16),
            pltpu.VMEM((2, NB, NB), jnp.float32),
            pltpu.VMEM((HOPS + 1, 3, 1, NG), jnp.int32),
            pltpu.VMEM((4, NQ, BLOCK, NB), jnp.float32),
            pltpu.VMEM((4, NQ, BLOCK, NB), jnp.float32),
            pltpu.VMEM((4, 2, HALF, NB), jnp.float32),
            pltpu.VMEM((3, 2, 2, HALF, NB), jnp.float32),
            pltpu.VMEM((2 * NQ, 32, NB), jnp.float32),
            dma((HOPS, CHUNKS)), dma((HOPS, CHUNKS)), dma, dma, dma((HOPS,)), dma((HOPS,)),
            dma((5, NQ)), dma((5, NQ)), dma((5, 3)), dma((3, 2, 2)),
            dma((NQ,)), dma((NQ,)), dma((NQ,)), dma((NQ,)), dma, dma,
            dma, pltpu.SemaphoreType.REGULAR((4,)),
        ],
        compiler_params=pltpu.CompilerParams(
            collective_id=0, has_side_effects=True, vmem_limit_bytes=48 * 1024 * 1024
        ),
        cost_estimate=pl.CostEstimate(
            flops=2 * 4 * 512 * NG * (NG + 512), bytes_accessed=4 * 512 * NG, transcendentals=0
        ),
    )(
        pltpu.with_memory_space_constraint(wave.reshape(2, 16, 16, NG), pltpu.HBM),
        pltpu.with_memory_space_constraint(wave.reshape(2, NQ, 2, 16, NG), pltpu.HBM),
        pltpu.with_memory_space_constraint(wave_perm[0][:, None, :], pltpu.HBM),
        pltpu.with_memory_space_constraint(shell_weight, pltpu.HBM),
    )
    return correlation[None], gradient[None]


def solution(mesh):
    placed = (P("ka", None, None, "pw"), P("ka", None, "pw"), P())
    return jax.shard_map(
        local,
        mesh=mesh,
        in_specs=placed,
        out_specs=(P("ka", None, None, "pw", None), P("ka", None, None, None)),
        check_vma=False,
    )
```

```python
import jax
import jax.numpy as jnp
from jax import lax
from jax.experimental import pallas as pl
from jax.experimental.pallas import tpu as pltpu
from jax.sharding import PartitionSpec as P

MESH = pl.DeviceIdType.MESH
NK = 32
NB = 256
NG = 1280
NQ = 8
HOPS = 4
CHUNKS = 4
ROWS = NB // CHUNKS
BLOCKS = ROWS // 16
A, B, W, C = range(4)
BLOCK = 72
HALF = 40


def kernel(
    wave_in, wave_halves, perm, weight_in, corr_out, grad_out,
    weight, wave, stream, other, turned, product, lists, part, gathered, reduced, ends, zrows,
    stream_send, stream_recv, other_send, other_recv, list_send, list_recv,
    part_send, part_recv, end_send, end_recv, z_send, z_recv, zz_send, zz_recv, wave_sem, list_sem, weight_sem, told,
):
    k = lax.axis_index("ka")
    p = lax.axis_index("pw")
    core = p % 2
    q = p // 2
    sibling = p + 1 - 2 * core
    level = k // 2 % 4
    group = k // 8 * 8
    inner = k % 8
    to_next = (k + 30 + 4 * core) % NK
    a_up, a_down = (k + 8) % NK, (k + 24) % NK
    b_up, b_down = group + (inner + 2) % 8, group + (inner + 6) % 8
    flip = k + 1 - 2 * (k % 2)
    a_end = (k + 8 + 16 * core) % NK
    b_end = group + (inner + 2 + 4 * core) % 8
    w_end = group + (inner + 6 - 4 * core) % 8
    b_here = level != 3 - 3 * core
    w_here = level == 3 * core

    def remote(src, dst, send_sem, recv_sem, ka, pw):
        return pltpu.make_async_remote_copy(
            src_ref=src, dst_ref=dst, send_sem=send_sem, recv_sem=recv_sem,
            device_id=(ka, pw), device_id_type=MESH,
        )

    around = [
        ((k + 2) % NK, p), ((k + 30) % NK, p), (flip, p), (flip, (q + 4) % NQ * 2 + core),
        (k, (q // 4 * 4 + (q + 1) % 4) * 2 + core), (k, (q // 4 * 4 + (q + 3) % 4) * 2 + core), (k, sibling),
    ]

    def tell(sem):
        for neighbour in around:
            pl.semaphore_signal(sem, inc=1, device_id=neighbour, device_id_type=MESH)

    barrier = pltpu.get_barrier_semaphore()
    tell(barrier)
    wave_copy = pltpu.make_async_copy(wave_in, wave, wave_sem)
    own_list_copy = pltpu.make_async_copy(perm, lists.at[0], list_sem)
    weight_copy = pltpu.make_async_copy(weight_in, weight, weight_sem)
    wave_copy.start()
    own_list_copy.start()
    weight_copy.start()
    pl.semaphore_wait(barrier, len(around))

    def blocks(c):
        return pl.ds(c * BLOCKS, BLOCKS)

    def own_copy(c, source):
        return remote(
            source, stream.at[0, :, blocks(c)],
            stream_send.at[0, c], stream_recv.at[0, c], to_next, p,
        )

    def hop_copy(h, c):
        return remote(
            stream.at[h - 1, :, blocks(c)], stream.at[h, :, blocks(c)],
            stream_send.at[h, c], stream_recv.at[h, c], to_next, p,
        )

    def list_copy(h):
        source = perm if h == 0 else lists.at[h]
        rows = slice(0, 1 if h == HOPS - 1 else 2)
        return remote(
            source.at[rows], lists.at[h + 1, rows], list_send.at[h], list_recv.at[h], to_next, p
        )

    other_copy = remote(wave_in, other, other_send, other_recv, flip, p)

    list_copy(0).start()

    @pl.when(core == 0)
    def _():
        for c in range(CHUNKS):
            own_copy(c, wave_in.at[:, blocks(c)]).start()

    @pl.when(core == 1)
    def _():
        for c in range(CHUNKS):
            own_copy(c, wave_halves.at[:, c % 2 * 4:c % 2 * 4 + 4, c // 2]).start()

    other_copy.start()
    tell(told.at[0])
    own_list_copy.wait()
    wave_copy.wait()
    weight_copy.wait()

    def turn_start(slot, direction):
        @pl.loop(0, NG // 256)
        def _(j):
            row = lists[0, direction] - p * NG
            wanted = lax.broadcasted_iota(jnp.int32, (256, NG), 0) + j * 256
            pick = jnp.where(wanted == row, 1.0, 0.0).astype(jnp.bfloat16)
            value = lax.dot_general(
                wave[...].reshape(2 * NB, NG), pick, (((1,), (1,)), ((), ())),
                preferred_element_type=jnp.float32,
            )
            turned[slot, :, pl.ds(pl.multiple_of(j * 256, 256), 256)] = value.astype(jnp.bfloat16)

    def turn_end(slot, direction, hops):
        @pl.loop(0, NG // 256)
        def _(j):
            columns = pl.ds(pl.multiple_of(j * 256, 256), 256)
            row = lists[hops, direction, :, columns] - p * NG
            held = lax.broadcasted_iota(jnp.int32, (NG, 256), 0)
            pick = jnp.where(held == row, 1.0, 0.0).astype(jnp.bfloat16)
            value = lax.dot_general(
                wave[...].reshape(2 * NB, NG), pick, (((1,), (0,)), ((), ())),
                preferred_element_type=jnp.float32,
            )
            turned[slot, :, columns] = value.astype(jnp.bfloat16)

    def multiply(slot, source, c, order):
        value = lax.dot_general(
            source[:, blocks(c)].reshape(2 * ROWS, NG), turned[slot], (((1,), (1,)), ((), ())),
            preferred_element_type=jnp.float32,
        )
        real = value[:ROWS, :NB] + value[ROWS:, NB:]
        imag = value[:ROWS, NB:] - value[ROWS:, :NB]
        for i in range(BLOCKS):
            n = c * BLOCKS + i
            block = n + order * (n % NQ * 2 + n // NQ - n)
            rows = pl.ds(pl.multiple_of(block * 16, 16), 16)
            product[0, rows, :] = real[16 * i:16 * i + 16]
            product[1, rows, :] = imag[16 * i:16 * i + 16]

    def part_copy(slot, j):
        dest = (q + j) % NQ
        return remote(
            part.at[slot, dest], gathered.at[slot, j],
            part_send.at[slot, j], part_recv.at[slot, j], k, dest * 2 + core,
        )

    def hand_out(slot, at_start):
        swap = jnp.broadcast_to(at_start, (NB, NB)) > 0
        real, imag = product[0], product[1]
        real = jnp.where(swap, real.T, real)
        imag = jnp.where(swap, -imag.T, imag)
        eye = lax.broadcasted_iota(jnp.int32, (NB, NB), 0) == lax.broadcasted_iota(jnp.int32, (NB, NB), 1)
        diag_real = jnp.sum(jnp.where(eye, real, 0.0), axis=0, keepdims=True)
        diag_imag = jnp.sum(jnp.where(eye, imag, 0.0), axis=0, keepdims=True)
        first = lax.broadcasted_iota(jnp.int32, (8, NB), 0) < 4
        diag = jnp.where(first, diag_real, diag_imag)
        real = real.reshape(NQ, 2, 16, NB)
        imag = imag.reshape(NQ, 2, 16, NB)
        part[slot, :, 0:16, :] = real[:, 0]
        part[slot, :, 16:32, :] = imag[:, 0]
        part[slot, :, 32:48, :] = real[:, 1]
        part[slot, :, 48:64, :] = imag[:, 1]
        part[slot, :, 64:72, :] = jnp.broadcast_to(diag[None], (NQ, 8, NB))

        @pl.loop(1, NQ)
        def _(j):
            part_copy(slot, j).start()

    def end_copies(slot):
        if slot == C:
            direction, role, far_role, end, near, far = 2, 0, 1, flip, core, core
        elif slot == W:
            direction, role, far_role, end, near, far = 1, 1 - core, core, w_end, 0, 1
        else:
            direction, role, far_role, end, near, far = 1, core, 1 - core, b_end, 0, 1
        local = (direction, role, near)
        target = ends.at[direction, far_role, far]
        sem = end_recv.at[direction, far_role, far]
        copies = [
            remote(
                reduced.at[slot, 1 - core], ends.at[direction, role, near],
                end_send.at[slot, 0], end_recv.at[direction, role, near], k, sibling,
            ),
            remote(reduced.at[slot, 0], target, end_send.at[slot, 1], sem, end, 2 * q),
            remote(reduced.at[slot, 1], target, end_send.at[slot, 2], sem, end, 2 * q + 1),
        ]
        return local, copies

    def pass_on(slot):
        @pl.loop(1, NQ)
        def _(j):
            part_copy(slot, j).wait_recv()

        total = part[slot, q]
        for j in range(1, NQ):
            total = total + gathered[slot, j]
        reduced[slot, 0, 0:32, :] = total[0:32]
        reduced[slot, 0, 32:40, :] = total[64:72]
        reduced[slot, 1, 0:32, :] = total[32:64]
        reduced[slot, 1, 32:40, :] = total[64:72]
        local, copies = end_copies(slot)
        for copy in copies:
            copy.start()
        ends[local[0], local[1], local[2]] = reduced[slot, core]

    def a_piece(ref, on, h):
        if on == 0:
            return ref.at[:, 128 * h:128 * h + 128]
        return ref.at[32 * h:(32, BLOCK)[h], :]

    def a_part_copy(on, h, j):
        dest = (q + j) % NQ
        row = (4, A)[h]
        return remote(
            a_piece(part.at[A, dest], on, h), a_piece(gathered.at[A, j], on, h),
            part_send.at[row, j], part_recv.at[row, j], k, dest * 2 + core,
        )

    def a_diag(real, imag, h):
        shape = real.shape
        eye = (
            lax.broadcasted_iota(jnp.int32, shape, 0) == lax.broadcasted_iota(jnp.int32, shape, 1) + 128 * h
        )
        diag_real = jnp.sum(jnp.where(eye, real, 0.0), axis=0, keepdims=True)
        diag_imag = jnp.sum(jnp.where(eye, imag, 0.0), axis=0, keepdims=True)
        first = lax.broadcasted_iota(jnp.int32, (8, shape[1]), 0) < 4
        return jnp.broadcast_to(jnp.where(first, diag_real, diag_imag)[None], (NQ, 8, shape[1]))

    def a_hand_out(h):
        @pl.when(core == 0)
        def _():
            columns = slice(128 * h, 128 * h + 128)
            real = product[0, columns, :].T
            imag = -product[1, columns, :].T
            part[A, :, 64:72, columns] = a_diag(real, imag, h)
            real = real.reshape(NQ, 2, 16, 128)
            imag = imag.reshape(NQ, 2, 16, 128)
            for i in range(2):
                part[A, :, 32 * i:32 * i + 16, columns] = real[:, i]
                part[A, :, 32 * i + 16:32 * i + 32, columns] = imag[:, i]

            @pl.loop(1, NQ)
            def _(j):
                a_part_copy(0, h, j).start()

        @pl.when(core == 1)
        def _():
            real, imag = product[0], product[1]
            if h == 1:
                part[A, :, 64:72, :] = a_diag(real, imag, 0)
            part[A, :, 32 * h:32 * h + 16, :] = real.reshape(NQ, 2, 16, NB)[:, h]
            part[A, :, 32 * h + 16:32 * h + 32, :] = imag.reshape(NQ, 2, 16, NB)[:, h]

            @pl.loop(1, NQ)
            def _(j):
                a_part_copy(1, h, j).start()

    def a_end_copies(on, h):
        near, near_sem = ends.at[0, on, 0], end_recv.at[0, on, 0]
        far, far_sem = ends.at[0, 1 - on, 1], end_recv.at[0, 1 - on, 1]
        row = (4, A)[h]
        if on == 0:
            rows, columns = slice(0, HALF), slice(128 * h, 128 * h + 128)
            last = [(1, near, near_sem, k, sibling), (1, far, far_sem, a_end, 2 * q + 1)]
            todo = last + [(0, far, far_sem, a_end, 2 * q)]
            cuts = [(rows, columns)] * 3
        else:
            rows, columns = slice(32 * h, (32, HALF)[h]), slice(0, NB)
            todo = [(0, near, near_sem, k, sibling), (0, far, far_sem, a_end, 2 * q)]
            cuts = [(rows, columns)] * 2
            if h == 1:
                todo = todo + [(1, far, far_sem, a_end, 2 * q + 1)]
                cuts = cuts + [(slice(0, HALF), columns)]
        return [
            remote(
                reduced.at[A, half, cut[0], cut[1]], target.at[cut[0], cut[1]],
                end_send.at[row, i], sem, ka, pw,
            )
            for i, ((half, target, sem, ka, pw), cut) in enumerate(zip(todo, cuts))
        ]

    def a_pass_on(h):
        for on in range(2):
            @pl.when(core == on)
            def _():
                @pl.loop(1, NQ)
                def _(j):
                    a_part_copy(on, h, j).wait_recv()

                total = a_piece(part.at[A, q], on, h)[...]
                for j in range(1, NQ):
                    total = total + a_piece(gathered.at[A, j], on, h)[...]
                if on == 0:
                    columns = slice(128 * h, 128 * h + 128)
                    for half in range(2):
                        reduced[A, half, 0:32, columns] = total[32 * half:32 * half + 32]
                        reduced[A, half, 32:40, columns] = total[64:72]
                else:
                    reduced[A, h, 0:32, :] = total[0:32]
                    if h == 1:
                        reduced[A, 0, 32:40, :] = total[32:40]
                        reduced[A, 1, 32:40, :] = total[32:40]
                for copy in a_end_copies(on, h):
                    copy.start()

        if h == 1:
            ends[0, core, 0] = reduced[A, core]

    turn_start(C, 2)
    list_copy(0).wait_recv()
    list_copy(1).start()
    for c in range(CHUNKS):
        own_copy(c, stream.at[0, :, blocks(c)]).wait_recv()
        hop_copy(1, c).start()
        pl.semaphore_wait(told.at[c], len(around))
        if c < CHUNKS - 1:
            tell(told.at[c + 1])

    @pl.when(b_here)
    def _():
        @pl.when(core == 0)
        def _():
            turn_start(B, 1)

        @pl.when(core == 1)
        def _():
            turn_end(B, 1, 1)

        @pl.loop(0, CHUNKS)
        def _(c):
            multiply(B, stream.at[0], c, core)

        hand_out(B, 1 - core)

    list_copy(1).wait_recv()
    list_copy(2).start()

    @pl.when(core == 0)
    def _():
        turn_start(A, 0)

    @pl.loop(0, CHUNKS)
    def _(c):
        hop_copy(1, c).wait_recv()
        hop_copy(2, c).start()

    other_copy.wait_recv()

    @pl.loop(0, CHUNKS)
    def _(c):
        multiply(C, other, c, 0)

    hand_out(C, 1)

    list_copy(2).wait_recv()
    list_copy(3).start()

    @pl.when(w_here)
    def _():
        @pl.when(core == 0)
        def _():
            turn_end(W, 1, 3)

        @pl.when(core == 1)
        def _():
            turn_start(W, 1)
    @pl.loop(0, CHUNKS)
    def _(c):
        hop_copy(2, c).wait_recv()
        hop_copy(3, c).start()

    @pl.when(w_here)
    def _():
        @pl.loop(0, CHUNKS)
        def _(c):
            multiply(W, stream.at[2], c, core)

        hand_out(W, core)

    pass_on(C)

    list_copy(3).wait_recv()

    @pl.when(core == 1)
    def _():
        turn_end(A, 0, 4)

    @pl.loop(0, CHUNKS // 2)
    def _(c):
        hop_copy(3, c).wait_recv()
        multiply(A, stream.at[3], c, core)

    a_hand_out(0)

    @pl.loop(CHUNKS // 2, CHUNKS)
    def _(c):
        hop_copy(3, c).wait_recv()
        multiply(A, stream.at[3], c, core)

    a_hand_out(1)

    a_pass_on(0)

    @pl.when(b_here)
    def _():
        pass_on(B)

    @pl.when(w_here)
    def _():
        pass_on(W)

    a_pass_on(1)

    def arrived(direction, role, place):
        ref = ends.at[direction, role, place]
        remote(ref, ref, end_send.at[A, 0], end_recv.at[direction, role, place], k, sibling).wait_recv()

    arrived(2, 0, 1 - core)
    arrived(2, 1, 0)
    arrived(2, 1, 1)
    arrived(1, 0, 1)
    arrived(1, 1, 1)

    @pl.when(core != level // 3)
    def _():
        arrived(1, 0, 0)

    @pl.when(core != (level + 2) // 3)
    def _():
        arrived(1, 1, 0)

    arrived(0, 1 - core, 0)
    arrived(0, 0, 1)
    arrived(0, 1, 1)

    z_real = jnp.zeros((16, NB), jnp.float32)
    z_imag = jnp.zeros((16, NB), jnp.float32)
    own_column = (
        lax.broadcasted_iota(jnp.int32, (16, NB), 0) + p * 16 == lax.broadcasted_iota(jnp.int32, (16, NB), 1)
    )
    for direction in range(3):
        ahead = ends[direction, 0, 0] + ends[direction, 0, 1]
        behind = ends[direction, 1, 0] + ends[direction, 1, 1]
        real, imag = ahead[0:16], ahead[16:32]
        diag_real, diag_imag = ahead[32:33], ahead[36:37]
        corr_out[direction, 0] = real
        corr_out[direction, 1] = imag
        back_real, back_imag = behind[0:16], behind[16:32]
        row_real = jnp.sum(jnp.where(own_column, back_real, 0.0), axis=1, keepdims=True)
        row_imag = jnp.sum(jnp.where(own_column, back_imag, 0.0), axis=1, keepdims=True)
        scale = weight[direction]
        z_real += scale * (
            real * diag_real + imag * diag_imag - (back_real * row_real + back_imag * row_imag)
        )
        z_imag += scale * (
            imag * diag_real - real * diag_imag - (back_imag * row_real - back_real * row_imag)
        )
    zrows[p, 0:16, :] = z_real
    zrows[p, 16:32, :] = z_imag

    def z_copy(j):
        dest = (q + j) % NQ * 2 + core
        return remote(zrows.at[p], zrows.at[p], z_send.at[j], z_recv.at[j], k, dest)

    def z_share(j):
        owner = (q + NQ - j) % NQ * 2 + core
        return remote(zrows.at[owner], zrows.at[owner], zz_send.at[j], zz_recv.at[j], k, sibling)

    @pl.loop(1, NQ)
    def _(j):
        z_copy(j).start()

    z_share(0).start()

    @pl.loop(1, NQ)
    def _(j):
        owner = (q + NQ - j) % NQ * 2 + core
        remote(zrows.at[owner], zrows.at[owner], z_send.at[j], z_recv.at[j], k, sibling).wait_recv()
        z_share(j).start()

    @pl.loop(0, NQ)
    def _(j):
        owner = (q + NQ - j) % NQ * 2 + 1 - core
        remote(zrows.at[owner], zrows.at[owner], zz_send.at[j], zz_recv.at[j], k, sibling).wait_recv()

    real = zrows[:, 0:16, :].reshape(NB, NB)
    imag = zrows[:, 16:32, :].reshape(NB, NB)
    grad_out[0] = 0.5 * (real - real.T)
    grad_out[1] = 0.5 * (imag + imag.T)

    for h in range(HOPS):
        list_copy(h).wait_send()
    other_copy.wait_send()

    @pl.loop(0, CHUNKS)
    def _(c):
        own_copy(c, stream.at[0, :, blocks(c)]).wait_send()
        for h in range(1, HOPS):
            hop_copy(h, c).wait_send()

    def sent(slot):
        @pl.loop(1, NQ)
        def _(j):
            part_copy(slot, j).wait_send()

        for copy in end_copies(slot)[1]:
            copy.wait_send()

    for on in range(2):
        @pl.when(core == on)
        def _():
            for h in range(2):
                @pl.loop(1, NQ)
                def _(j):
                    a_part_copy(on, h, j).wait_send()

                for copy in a_end_copies(on, h):
                    copy.wait_send()

    sent(C)

    @pl.when(b_here)
    def _():
        sent(B)

    @pl.when(w_here)
    def _():
        sent(W)

    z_share(0).wait_send()

    @pl.loop(1, NQ)
    def _(j):
        z_copy(j).wait_send()
        z_share(j).wait_send()


def local(wave, wave_perm, shell_weight):
    dma = pltpu.SemaphoreType.DMA
    vmem = pl.BlockSpec(memory_space=pltpu.VMEM)
    correlation, gradient = pl.pallas_call(
        kernel,
        out_shape=(
            jax.ShapeDtypeStruct((3, 2, 16, NB), jnp.float32),
            jax.ShapeDtypeStruct((2, NB, NB), jnp.float32),
        ),
        in_specs=[pl.BlockSpec(memory_space=pl.ANY)] * 4,
        out_specs=(vmem, vmem),
        scratch_shapes=[
            pltpu.SMEM((3,), jnp.float32),
            pltpu.VMEM((2, 16, 16, NG), jnp.bfloat16),
            pltpu.VMEM((HOPS, 2, 16, 16, NG), jnp.bfloat16),
            pltpu.VMEM((2, 16, 16, NG), jnp.bfloat16),
            pltpu.VMEM((4, 2 * NB, NG), jnp.bfloat16),
            pltpu.VMEM((2, NB, NB), jnp.float32),
            pltpu.VMEM((HOPS + 1, 3, 1, NG), jnp.int32),
            pltpu.VMEM((4, NQ, BLOCK, NB), jnp.float32),
            pltpu.VMEM((4, NQ, BLOCK, NB), jnp.float32),
            pltpu.VMEM((4, 2, HALF, NB), jnp.float32),
            pltpu.VMEM((3, 2, 2, HALF, NB), jnp.float32),
            pltpu.VMEM((2 * NQ, 32, NB), jnp.float32),
            dma((HOPS, CHUNKS)), dma((HOPS, CHUNKS)), dma, dma, dma((HOPS,)), dma((HOPS,)),
            dma((5, NQ)), dma((5, NQ)), dma((5, 3)), dma((3, 2, 2)),
            dma((NQ,)), dma((NQ,)), dma((NQ,)), dma((NQ,)), dma, dma,
            dma, pltpu.SemaphoreType.REGULAR((4,)),
        ],
        compiler_params=pltpu.CompilerParams(
            collective_id=0, has_side_effects=True, vmem_limit_bytes=48 * 1024 * 1024
        ),
        cost_estimate=pl.CostEstimate(
            flops=2 * 4 * 512 * NG * (NG + 512), bytes_accessed=4 * 512 * NG, transcendentals=0
        ),
    )(
        pltpu.with_memory_space_constraint(wave.reshape(2, 16, 16, NG), pltpu.HBM),
        pltpu.with_memory_space_constraint(wave.reshape(2, NQ, 2, 16, NG), pltpu.HBM),
        pltpu.with_memory_space_constraint(wave_perm[0][:, None, :], pltpu.HBM),
        pltpu.with_memory_space_constraint(shell_weight, pltpu.HBM),
    )
    return correlation[None], gradient[None]


def solution(mesh):
    placed = (P("ka", None, None, "pw"), P("ka", None, "pw"), P())
    return jax.shard_map(
        local,
        mesh=mesh,
        in_specs=placed,
        out_specs=(P("ka", None, None, "pw", None), P("ka", None, None, None)),
        check_vma=False,
    )
```
